128 devices in a mesh: seq: 16 (over z, y_hi, core), blk: 8 (over y_lo, x).
Axes of the slice: x: 4, y: 4 (y_hi: 2, y_lo: 2; y = y_hi * 2 + y_lo), z: 4, core: 2. Of those that a mesh axis runs over, the one named last changes fastest.
Arguments:
- tokens: bfloat16 [16384, 8192], P('seq', 'blk'), may hold values from -6 to 6
- right_factor: bfloat16 [64, 128, 128], P('blk', 'seq'), may hold values from -0.5 to 0.5
- left_factor: bfloat16 [128, 64, 64], P('blk', 'seq'), may hold values from -0.75 to 0.75
- target: bfloat16 [16384, 8192], P('seq', 'blk'), may hold values from -4 to 4
Outputs:
- student: bfloat16 [16384, 8192], P('seq', 'blk')
- right_grad: float32 [64, 128, 128], P('blk', 'seq')
- left_grad: float32 [128, 64, 64], P('blk', 'seq')
The draws below stay inside these ranges and needn't reach their ends.
All inputs are finite; a program needn't handle non-finite values.
Results may differ from the reference program's by a relative error of at most 0.017.
Values may be sent and summed in bfloat16 or wider, within the bound.
No kernel may reach another device: no remote copies, remote signals or barrier semaphores. Data moves between devices by JAX's collectives and lax.ppermute only.
A program may use at most 64 MiB of HBM per device.

```python
import jax
import jax.numpy as jnp

D = 8192
BLOCK = 128
NBLOCKS = 64
TOKENS = 16384


def levels(own_key, dims, split, smallest, largest):
    level = 1.0
    for position, parts in split:
        heights = jax.random.uniform(jax.random.fold_in(jax.random.fold_in(own_key, 6), position), (parts,), jnp.float32, smallest / len(split), largest / len(split))
        level = level * jnp.repeat(jnp.exp(heights), dims[position] // parts).reshape((-1,) + (1,) * (len(dims) - 1 - position))
    return level


def noise(stream_key, extent, scale, bound, shards=(), dtype=jnp.bfloat16):
    drawn = scale * jax.random.normal(stream_key, extent, jnp.float32)
    if shards:
        drawn = drawn * levels(stream_key, extent, shards, -0.22, 0.18)
    return jnp.clip(drawn, -bound, bound).astype(dtype)


def setup_inputs(seed: int = 0) -> dict:
    keys = jax.random.split(jax.random.key(seed), 5)
    return {
        "tokens": noise(keys[0], (TOKENS, D), 1.0, 6.0, ((0, 16), (1, 8))),
        "right_factor": noise(keys[1], (NBLOCKS, BLOCK, BLOCK), BLOCK ** -0.5, 0.5, ((0, 8), (1, 16))),
        "left_factor": noise(keys[2], (BLOCK, NBLOCKS, NBLOCKS), NBLOCKS ** -0.5, 0.75, ((0, 8), (1, 16))),
        "target": noise(keys[3], (TOKENS, D), 0.5, 4.0, ((0, 16), (1, 8))),
    }


def gelu_tanh(values):
    return jax.nn.gelu(values, approximate=True)

def reference(tokens, right_factor, left_factor, target):
    count = tokens.shape[0]
    scale = 1.0 / jnp.sqrt(jnp.float32(count))
    inputs = tokens.reshape(count, NBLOCKS, BLOCK).astype(jnp.float32)
    mixed = jnp.einsum('tki,kci->tkc', inputs, right_factor.astype(jnp.float32)).astype(jnp.bfloat16)
    turned = jnp.transpose(mixed, (0, 2, 1)).astype(jnp.float32)
    left_wide = left_factor.astype(jnp.float32)
    pre = jnp.einsum('tck,cmk->tcm', turned, left_wide)
    act, back = jax.vjp(gelu_tanh, pre)
    student = act.reshape(count, D).astype(jnp.bfloat16)
    residual = (act - target.reshape(count, BLOCK, NBLOCKS).astype(jnp.float32)) * scale
    pre_grad = back(residual)[0].astype(jnp.bfloat16).astype(jnp.float32)
    turned_grad = jnp.einsum('tcm,cmk->tck', pre_grad, left_wide).astype(jnp.bfloat16).astype(jnp.float32)
    left_grad = jnp.einsum('tcm,tck->cmk', pre_grad, turned)
    right_grad = jnp.einsum('tck,tki->kci', turned_grad, inputs)
    return (student, right_grad, left_grad)
```

```python
import functools
import math

import jax
import jax.numpy as jnp
from jax import lax
from jax.experimental import pallas as pl
from jax.experimental.pallas import tpu as pltpu
from jax.sharding import PartitionSpec as P

BF = jnp.bfloat16
F32 = jnp.float32
MIB = 1 << 20
ROOT = math.sqrt(2.0 / math.pi)
CUBE = 0.044715


def iota(shape, dim):
    return lax.broadcasted_iota(jnp.int32, shape, dim)


def cost(flops, size):
    return pl.CostEstimate(flops=int(flops), bytes_accessed=int(size), transcendentals=0)


def dot(a, b, dims=((1,), (0,))):
    return lax.dot_general(a, b, (dims, ((), ())), preferred_element_type=F32)


def params(limit=24):
    return pltpu.CompilerParams(vmem_limit_bytes=limit * MIB)


def mix_kernel(x_ref, g_ref, out_ref, big_ref):
    width = 1024

    @pl.when(pl.program_id(0) == 0)
    def _():
        flat = jnp.concatenate([g_ref[s, 0:64, :].astype(F32) for s in range(16)], axis=0)
        turned = flat.T
        lane_k = (iota((128, width), 1) >> 3) & 7
        for k in range(8):
            big_ref[k * 128 : (k + 1) * 128, :] = jnp.where(lane_k == k, turned, 0.0).astype(BF)

    mixed = dot(x_ref[...], big_ref[...]).astype(BF)
    for j in range(8):
        out_ref[j] = mixed[:, j * 128 : (j + 1) * 128]


def mix(x, gathered):
    rows = x.shape[0]
    step = 256
    return pl.pallas_call(
        mix_kernel,
        grid=(rows // step,),
        in_specs=[
            pl.BlockSpec((step, 1024), lambda t: (t, 0)),
            pl.BlockSpec((16, 96, 128), lambda t: (0, 0, 0)),
        ],
        out_specs=pl.BlockSpec((8, step, 128), lambda t: (0, t, 0)),
        out_shape=jax.ShapeDtypeStruct((8, rows, 128), BF),
        scratch_shapes=[pltpu.VMEM((1024, 1024), BF)],
        compiler_params=params(),
        cost_estimate=cost(2 * rows * 1024 * 1024, 4 * rows * 1024),
        name="mix",
    )(x, gathered)


def permutation():
    r, q = iota((512, 512), 0), iota((512, 512), 1)
    here = ((r >> 6) == ((q >> 2) & 7)) & (((r >> 2) & 15) == (q >> 5)) & ((r & 3) == (q & 3))
    return here.astype(F32).astype(BF)


def spread(h):
    r, f = iota((128, 1024), 0), iota((128, 1024), 1)
    k = ((f >> 7) << 3) + ((f >> 3) & 7)
    return (r == k + h * 64).astype(F32).astype(BF)


def column_block(f):
    return (((f >> 6) & 1) << 3) + (f & 7)


def expand_kernel(g_ref, wide_ref, back_ref):
    packed = jnp.concatenate([g_ref[s, 64:96, :] for s in range(16)], axis=0)
    ordered = dot(permutation(), packed)
    turned = ordered.T.astype(BF)
    ordered = ordered.astype(BF)
    for h in range(2):
        once = spread(h)
        row_c = (iota((512, 1024), 0) >> 6) + h * 8
        match = row_c == column_block(iota((512, 1024), 1))
        back_ref[h * 512 : (h + 1) * 512, :] = jnp.where(match, dot(ordered, once), 0.0).astype(BF)
        col_c = (iota((1024, 512), 1) >> 6) + h * 8
        match = col_c == column_block(iota((1024, 512), 0))
        full = dot(once, turned, ((0,), (0,)))
        wide_ref[:, h * 512 : (h + 1) * 512] = jnp.where(match, full, 0.0).astype(BF)


def expand(gathered):
    shape = jax.ShapeDtypeStruct((1024, 1024), BF)
    return pl.pallas_call(
        expand_kernel,
        out_shape=(shape, shape),
        compiler_params=params(40),
        cost_estimate=cost(2 * 1024 * 1024 * 1024, 4 * MIB),
        name="expand",
    )(gathered)


def turn_kernel(x_ref, out_ref):
    out_ref[...] = x_ref[...].T


def turn(x):
    rows, width = x.shape
    step = 256
    return pl.pallas_call(
        turn_kernel,
        grid=(width // step,),
        in_specs=[pl.BlockSpec((rows, step), lambda f: (0, f))],
        out_specs=pl.BlockSpec((step, rows), lambda f: (f, 0)),
        out_shape=jax.ShapeDtypeStruct((width, rows), BF),
        compiler_params=params(),
        cost_estimate=cost(2 * rows * 1024 * 1024, 4 * rows * 1024),
        name="turn",
    )(x)


def middle_kernel(scale, in_ref, wide_ref, back_ref, target_ref, student_ref, grad_ref, out_ref):
    turned = jnp.concatenate([in_ref[j] for j in range(8)], axis=1)
    v = dot(turned, wide_ref[...])
    square = v * v
    p = 0.5 + 0.5 * jnp.tanh(v * (ROOT + (ROOT * CUBE) * square))
    act = v * p
    slope = p + (act - act * p) * (2.0 * ROOT + (6.0 * ROOT * CUBE) * square)
    student_ref[...] = act.astype(BF)
    grad = ((act - target_ref[...].astype(F32)) * (slope * scale)).astype(BF)
    grad_ref[...] = grad
    out = dot(grad, back_ref[...]).astype(BF)
    for j in range(8):
        out_ref[j] = out[:, j * 128 : (j + 1) * 128]


def middle(received, wide, back, target, scale):
    rows = target.shape[0]
    step = 256
    block = pl.BlockSpec((8, step, 128), lambda t: (0, t, 0))
    line = pl.BlockSpec((step, 1024), lambda t: (t, 0))
    whole = pl.BlockSpec((1024, 1024), lambda t: (0, 0))
    flat = jax.ShapeDtypeStruct((rows, 1024), BF)
    return pl.pallas_call(
        functools.partial(middle_kernel, scale),
        grid=(rows // step,),
        in_specs=[block, whole, whole, line],
        out_specs=(line, line, block),
        out_shape=(flat, flat, jax.ShapeDtypeStruct((8, rows, 128), BF)),
        compiler_params=params(40),
        cost_estimate=cost(4 * rows * 1024 * 1024, 10 * rows * 1024),
        name="middle",
    )(received, wide, back, target)


def left_kernel(grad_ref, in_ref, out_ref, total_ref):
    step = pl.program_id(0)
    h = step // 2
    turned = jnp.concatenate([in_ref[j] for j in range(8)], axis=1)
    full = dot(grad_ref[...], turned, ((0,), (0,)))
    row_c = (iota((256, 1024), 0) >> 6) + step * 4
    full = jnp.where(row_c == column_block(iota((256, 1024), 1)), full, 0.0).astype(BF)
    kept = dot(full, spread(h), ((1,), (1,)))
    place = pl.ds(pl.multiple_of((step % 2) * 256, 256), 256)

    @pl.when(step < 2)
    def _():
        total_ref[place, :] = kept

    @pl.when(step >= 2)
    def _():
        total_ref[place, :] += kept

    @pl.when(step == 3)
    def _():
        ordered = dot(permutation(), total_ref[...].astype(BF), ((0,), (0,))).astype(BF)
        for s in range(16):
            out_ref[s] = ordered[s * 32 : (s + 1) * 32, :]


def left_grads(grad, received):
    rows = grad.shape[0]
    return pl.pallas_call(
        left_kernel,
        grid=(4,),
        in_specs=[
            pl.BlockSpec((rows, 256), lambda n: (0, n)),
            pl.BlockSpec((8, rows, 128), lambda n: (0, 0, 0)),
        ],
        out_specs=pl.BlockSpec((16, 32, 128), lambda n: (0, 0, 0)),
        out_shape=jax.ShapeDtypeStruct((16, 32, 128), BF),
        scratch_shapes=[pltpu.VMEM((512, 128), F32)],
        compiler_params=params(40),
        cost_estimate=cost(4 * rows * 1024 * 1024, 4 * rows * 1024),
        name="left_grads",
    )(grad, received)


def right_kernel(in_ref, turned_ref, left_ref, out_ref):
    pair = jnp.concatenate([in_ref[0], in_ref[1]], axis=1)
    full = dot(turned_ref[...], pair)
    lane_k = (iota((128, 256), 1) >> 3) & 7
    kept = jnp.zeros((128, 256), F32)
    for k in range(8):
        kept = jnp.where(lane_k == k, full[k * 128 : (k + 1) * 128, :], kept)
    kept = kept.T.astype(BF)
    for s in range(4):
        out_ref[s, 0:64, :] = kept[s * 64 : (s + 1) * 64, :]
        out_ref[s, 64:96, :] = left_ref[s]


def right_grads(received, turned, left):
    rows = turned.shape[1]
    return pl.pallas_call(
        right_kernel,
        grid=(4,),
        in_specs=[
            pl.BlockSpec((2, rows, 128), lambda n: (n, 0, 0)),
            pl.BlockSpec((1024, rows), lambda n: (0, 0)),
            pl.BlockSpec((4, 32, 128), lambda n: (n, 0, 0)),
        ],
        out_specs=pl.BlockSpec((4, 96, 128), lambda n: (n, 0, 0)),
        out_shape=jax.ShapeDtypeStruct((16, 96, 128), BF),
        compiler_params=params(40),
        cost_estimate=cost(2 * rows * 1024 * 1024, 4 * rows * 1024),
        name="right_grads",
    )(received, turned, left)


def shards(tokens, right_factor, left_factor, target):
    rows = tokens.shape[0]
    scale = 1.0 / math.sqrt(rows * lax.axis_size("seq"))
    packed = jnp.concatenate(
        [
            right_factor.reshape(64, 128),
            jnp.concatenate([left_factor[:8], left_factor[8:]], axis=2).reshape(32, 128),
        ],
        axis=0,
    )
    gathered = lax.all_to_all(jnp.broadcast_to(packed, (16, 96, 128)), "seq", 0, 0, tiled=True)
    mixed = mix(tokens, gathered)
    received = lax.all_to_all(mixed, "blk", 0, 0, tiled=True)
    wide, back = expand(gathered)
    turned = turn(tokens)
    student, grad, out = middle(received, wide, back, target, scale)
    returned = lax.all_to_all(out, "blk", 0, 0, tiled=True)
    left = left_grads(grad, received)
    terms = right_grads(returned, turned, left)
    terms = lax.all_to_all(terms, "seq", 0, 0, tiled=True)
    total = jnp.sum(terms.astype(F32), axis=0)
    right_grad = total[:64].reshape(8, 8, 128)
    left_total = total[64:].reshape(8, 4, 2, 64)
    left_grad = jnp.transpose(left_total, (2, 0, 1, 3)).reshape(16, 4, 64)
    return (student, right_grad, left_grad)


def solution(mesh):
    return jax.shard_map(
        shards,
        mesh=mesh,
        in_specs=(P("seq", "blk"), P("blk", "seq", None), P("blk", "seq", None), P("seq", "blk")),
        out_specs=(P("seq", "blk"), P("blk", "seq", None), P("blk", "seq", None)),
        check_vma=False,
    )
```

```python
import functools
import math

import jax
import jax.numpy as jnp
from jax import lax
from jax.experimental import pallas as pl
from jax.experimental.pallas import tpu as pltpu
from jax.sharding import PartitionSpec as P

BF = jnp.bfloat16
F32 = jnp.float32
MIB = 1 << 20
ROOT = math.sqrt(2.0 / math.pi)
CUBE = 0.044715


def iota(shape, dim):
    return lax.broadcasted_iota(jnp.int32, shape, dim)


def dot(a, b, dims=((1,), (0,))):
    return lax.dot_general(a, b, (dims, ((), ())), preferred_element_type=F32)


def params(limit=24):
    return pltpu.CompilerParams(vmem_limit_bytes=limit * MIB)


def cost(flops, size):
    return pl.CostEstimate(flops=int(flops), bytes_accessed=int(size), transcendentals=0)


def parity():
    return lax.rem(lax.axis_index("blk"), 2)


def joined(parts):
    return jnp.concatenate(parts, axis=1)


def halves(blocks):
    low = iota(blocks[0].shape, 1) < 64
    first = joined([jnp.where(low, blocks[2 * p], blocks[2 * p + 1]) for p in range(4)])
    second = joined([jnp.where(low, blocks[2 * p + 1], blocks[2 * p]) for p in range(4)])
    return first, second


def split(blocks):
    even = ((iota(blocks[0].shape, 1) >> 5) & 1) == 0
    first = joined([jnp.where(even, blocks[2 * p], blocks[2 * p + 1]) for p in range(4)])
    second = joined([jnp.where(even, blocks[2 * p + 1], blocks[2 * p]) for p in range(4)])
    return first, second


def source(pair, g, kh, par):
    return 2 * (2 * pair + ((g & 1) ^ kh)) + ((g >> 1) ^ par)


def pack_kernel(right_ref, left_ref, out_ref):
    right = right_ref[...].astype(F32).reshape(64, 128)
    left = left_ref[...].astype(F32).reshape(64, 64)
    whole = jnp.concatenate([right, joined([left[:32], left[32:]])], axis=0).astype(BF)
    for s in range(16):
        out_ref[s] = whole


def pack(right, left):
    return pl.pallas_call(
        pack_kernel,
        out_shape=jax.ShapeDtypeStruct((16, 96, 128), BF),
        compiler_params=params(),
        name="pack",
    )(right, left)


def permutation():
    r, q = iota((512, 512), 0), iota((512, 512), 1)
    here = ((r >> 6) == ((q >> 2) & 7)) & (((r >> 2) & 15) == (q >> 5)) & ((r & 3) == (q & 3))
    return here.astype(F32).astype(BF)


def spread(h, par):
    r, f = iota((128, 512), 0), iota((128, 512), 1)
    device = ((f >> 7) << 1) + (((f >> 6) & 1) ^ h)
    k = (device << 3) + ((((f >> 5) & 1) ^ par) << 2) + ((f >> 3) & 3)
    return (r == k + h * 64).astype(F32).astype(BF)


def same_block(shape):
    return (iota(shape, 0) >> 6) == (iota(shape, 1) & 7)


def mix_kernel(x_ref, g_ref, out_ref, back_ref, big_ref):
    @pl.when(pl.program_id(0) == 0)
    def _():
        par = parity()
        lane_k = (iota((128, 512), 1) >> 3) & 3
        for kh in range(2):
            rows = [
                g_ref[source(p, g, kh, par), kh * 32 : kh * 32 + 32, :].astype(F32)
                for p in range(4)
                for g in range(4)
            ]
            turned = jnp.concatenate(rows, axis=0).T
            for k in range(4):
                big_ref[kh, k * 128 : (k + 1) * 128, :] = jnp.where(lane_k == k, turned, 0.0).astype(BF)
        packed = jnp.concatenate([g_ref[s, 64:96, :] for s in range(16)], axis=0)
        ordered = dot(permutation(), packed).astype(BF)
        for h in range(2):
            full = dot(ordered, spread(h, par))
            back_ref[h] = jnp.where(same_block((512, 512)), full, 0.0).astype(BF)

    first = dot(x_ref[:, :512], big_ref[0]).astype(BF)
    second = dot(x_ref[:, 512:], big_ref[1]).astype(BF)
    even = ((iota((first.shape[0], 128), 1) >> 5) & 1) == 0
    for p in range(4):
        lanes = slice(p * 128, (p + 1) * 128)
        a, b = first[:, lanes], second[:, lanes]
        out_ref[2 * p] = jnp.where(even, a, b)
        out_ref[2 * p + 1] = jnp.where(even, b, a)


def mix(x, gathered):
    rows = x.shape[0]
    step = 256
    return pl.pallas_call(
        mix_kernel,
        grid=(rows // step,),
        in_specs=[
            pl.BlockSpec((step, 1024), lambda t: (t, 0)),
            pl.BlockSpec((16, 96, 128), lambda t: (0, 0, 0)),
        ],
        out_specs=(
            pl.BlockSpec((8, step, 128), lambda t: (0, t, 0)),
            pl.BlockSpec((2, 512, 512), lambda t: (0, 0, 0)),
        ),
        out_shape=(
            jax.ShapeDtypeStruct((8, rows, 128), BF),
            jax.ShapeDtypeStruct((2, 512, 512), BF),
        ),
        scratch_shapes=[pltpu.VMEM((2, 512, 512), BF)],
        compiler_params=params(),
        cost_estimate=cost(rows * 1024 * 1024, 4 * rows * 1024),
        name="mix",
    )(x, gathered)


def middle_kernel(scale, in_ref, back_ref, target_ref, student_ref, grad_ref, out_ref):
    turned = halves([in_ref[j] for j in range(8)])
    outs = []
    for h in range(2):
        lanes = slice(h * 512, (h + 1) * 512)
        v = dot(turned[h], back_ref[h], ((1,), (1,)))
        square = v * v
        p = 0.5 + 0.5 * jnp.tanh(v * (ROOT + (ROOT * CUBE) * square))
        act = v * p
        slope = p + (act - act * p) * (2.0 * ROOT + (6.0 * ROOT * CUBE) * square)
        student_ref[:, lanes] = act.astype(BF)
        grad = ((act - target_ref[:, lanes].astype(F32)) * (slope * scale)).astype(BF)
        grad_ref[:, lanes] = grad
        outs.append(dot(grad, back_ref[h]).astype(BF))
    low = iota((outs[0].shape[0], 128), 1) < 64
    for p in range(4):
        lanes = slice(p * 128, (p + 1) * 128)
        a, b = outs[0][:, lanes], outs[1][:, lanes]
        out_ref[2 * p] = jnp.where(low, a, b)
        out_ref[2 * p + 1] = jnp.where(low, b, a)


def middle(received, back, target, scale):
    rows = target.shape[0]
    step = 256
    block = pl.BlockSpec((8, step, 128), lambda t: (0, t, 0))
    line = pl.BlockSpec((step, 1024), lambda t: (t, 0))
    whole = pl.BlockSpec((2, 512, 512), lambda t: (0, 0, 0))
    flat = jax.ShapeDtypeStruct((rows, 1024), BF)
    return pl.pallas_call(
        functools.partial(middle_kernel, scale),
        grid=(rows // step,),
        in_specs=[block, whole, line],
        out_specs=(line, line, block),
        out_shape=(flat, flat, jax.ShapeDtypeStruct((8, rows, 128), BF)),
        compiler_params=params(),
        cost_estimate=cost(2 * rows * 1024 * 1024, 10 * rows * 1024),
        name="middle",
    )(received, back, target)


def grads_kernel(grad_ref, in_ref, back_ref, x_ref, out_ref):
    par = parity()
    turned = halves([in_ref[j] for j in range(8)])
    total = jnp.zeros((512, 128), F32)
    for h in range(2):
        full = dot(grad_ref[:, h * 512 : (h + 1) * 512], turned[h], ((0,), (0,)))
        full = jnp.where(same_block((512, 512)), full, 0.0).astype(BF)
        total = total + dot(full, spread(h, par), ((1,), (1,)))
    ordered = dot(permutation(), total.astype(BF), ((0,), (0,))).astype(BF)
    for s in range(16):
        out_ref[s, 64:96, :] = ordered[s * 32 : (s + 1) * 32, :]

    returned = split([back_ref[j] for j in range(8)])
    lane_k = (iota((128, 512), 1) >> 3) & 3
    for kh in range(2):
        full = dot(x_ref[:, kh * 512 : (kh + 1) * 512], returned[kh], ((0,), (0,)))
        kept = jnp.zeros((128, 512), F32)
        for k in range(4):
            kept = jnp.where(lane_k == k, full[k * 128 : (k + 1) * 128, :], kept)
        kept = kept.T.astype(BF)
        for p in range(4):
            for g in range(4):
                n = (p * 4 + g) * 32
                out_ref[source(p, g, kh, par), kh * 32 : kh * 32 + 32, :] = kept[n : n + 32, :]


def grads(grad, received, returned, x):
    rows = grad.shape[0]
    return pl.pallas_call(
        grads_kernel,
        out_shape=jax.ShapeDtypeStruct((16, 96, 128), BF),
        compiler_params=params(),
        cost_estimate=cost(2 * rows * 1024 * 1024, 8 * rows * 1024),
        name="grads",
    )(grad, received, returned, x)


def sum_kernel(in_ref, right_ref, left_ref):
    total = in_ref[0].astype(F32)
    for s in range(1, 16):
        total = total + in_ref[s].astype(F32)
    right_ref[...] = total[:64].reshape(8, 8, 128)
    left = total[64:]
    left_ref[:8] = left[:, :64].reshape(8, 4, 64)
    left_ref[8:] = left[:, 64:].reshape(8, 4, 64)


def sums(terms):
    return pl.pallas_call(
        sum_kernel,
        out_shape=(
            jax.ShapeDtypeStruct((8, 8, 128), F32),
            jax.ShapeDtypeStruct((16, 4, 64), F32),
        ),
        compiler_params=params(),
        name="sums",
    )(terms)


def shards(tokens, right_factor, left_factor, target):
    rows = tokens.shape[0]
    scale = 1.0 / math.sqrt(rows * lax.axis_size("seq"))
    gathered = lax.all_to_all(pack(right_factor, left_factor), "seq", 0, 0, tiled=True)
    mixed, back = mix(tokens, gathered)
    received = lax.all_to_all(mixed, "blk", 0, 0, tiled=True)
    student, grad, out = middle(received, back, target, scale)
    returned = lax.all_to_all(out, "blk", 0, 0, tiled=True)
    terms = grads(grad, received, returned, tokens)
    terms = lax.all_to_all(terms, "seq", 0, 0, tiled=True)
    right_grad, left_grad = sums(terms)
    return (student, right_grad, left_grad)


def solution(mesh):
    return jax.shard_map(
        shards,
        mesh=mesh,
        in_specs=(P("seq", "blk"), P("blk", "seq", None), P("blk", "seq", None), P("seq", "blk")),
        out_specs=(P("seq", "blk"), P("blk", "seq", None), P("blk", "seq", None)),
        check_vma=False,
    )
```

```python
import functools
import math

import jax
import jax.numpy as jnp
from jax import lax
from jax.experimental import pallas as pl
from jax.experimental.pallas import tpu as pltpu
from jax.sharding import PartitionSpec as P

BF = jnp.bfloat16
F32 = jnp.float32
MIB = 1 << 20
ROOT = math.sqrt(2.0 / math.pi)
CUBE = 0.044715


def iota(shape, dim):
    return lax.broadcasted_iota(jnp.int32, shape, dim)


def dot(a, b, dims=((1,), (0,))):
    return lax.dot_general(a, b, (dims, ((), ())), preferred_element_type=F32)


def params(limit=24):
    return pltpu.CompilerParams(vmem_limit_bytes=limit * MIB)


def cost(flops, size):
    return pl.CostEstimate(flops=int(flops), bytes_accessed=int(size), transcendentals=0)


def in_hbm(x):
    return pltpu.with_memory_space_constraint(x, pltpu.HBM)


def parity():
    return lax.rem(lax.axis_index("blk"), 2)


def joined(parts):
    return jnp.concatenate(parts, axis=1)


def halves(blocks):
    low = iota(blocks[0].shape, 1) < 64
    first = joined([jnp.where(low, blocks[2 * p], blocks[2 * p + 1]) for p in range(4)])
    second = joined([jnp.where(low, blocks[2 * p + 1], blocks[2 * p]) for p in range(4)])
    return first, second


def split(blocks):
    even = ((iota(blocks[0].shape, 1) >> 5) & 1) == 0
    first = joined([jnp.where(even, blocks[2 * p], blocks[2 * p + 1]) for p in range(4)])
    second = joined([jnp.where(even, blocks[2 * p + 1], blocks[2 * p]) for p in range(4)])
    return first, second


def source(pair, g, kh, par):
    return 2 * (2 * pair + ((g & 1) ^ kh)) + ((g >> 1) ^ par)


def pack_kernel(right_hbm, left_hbm, out_ref, right_ref, left_ref, sems):
    copies = [
        pltpu.make_async_copy(right_hbm, right_ref, sems.at[0]),
        pltpu.make_async_copy(left_hbm, left_ref, sems.at[1]),
    ]
    for copy in copies:
        copy.start()
    for copy in copies:
        copy.wait()
    right = right_ref[...].astype(F32).reshape(64, 128)
    left = left_ref[...].astype(F32).reshape(64, 64)
    whole = jnp.concatenate([right, joined([left[:32], left[32:]])], axis=0).astype(BF)
    for s in range(16):
        out_ref[s] = whole


def pack(right, left):
    return pl.pallas_call(
        pack_kernel,
        in_specs=[pl.BlockSpec(memory_space=pltpu.HBM)] * 2,
        out_shape=jax.ShapeDtypeStruct((16, 96, 128), BF),
        scratch_shapes=[
            pltpu.VMEM(right.shape, BF),
            pltpu.VMEM(left.shape, BF),
            pltpu.SemaphoreType.DMA((2,)),
        ],
        compiler_params=params(),
        name="pack",
    )(in_hbm(right), in_hbm(left))


def exchange(x, a, b):
    low = iota((8, x.shape[1]), 0) < 4

    def tile(i, j):
        n = (i * b + j) * 4
        return x[n : n + 8]

    parts = []
    for j in range(0, b, 2):
        pairs = [(tile(i, j), tile(i + 1, j)) for i in range(0, a, 2)]
        parts += [jnp.where(low, u, pltpu.roll(v, 4, 0)) for u, v in pairs]
        parts += [jnp.where(low, pltpu.roll(u, 4, 0), v) for u, v in pairs]
    return jnp.concatenate(parts, axis=0)


def spread(h, par):
    r, f = iota((128, 512), 0), iota((128, 512), 1)
    device = ((f >> 7) << 1) + (((f >> 6) & 1) ^ h)
    k = (device << 3) + ((((f >> 5) & 1) ^ par) << 2) + ((f >> 3) & 3)
    return (r == k + h * 64).astype(F32).astype(BF)


def same_block(shape):
    return (iota(shape, 0) >> 6) == (iota(shape, 1) & 7)


def mix_kernel(x_hbm, g_ref, out_ref, back_ref, x_ref, sems):
    copies = []
    for kh in range(2):
        lanes = slice(kh * 512, (kh + 1) * 512)
        copies.append(pltpu.make_async_copy(x_hbm.at[:, lanes], x_ref.at[kh], sems.at[kh]))
        copies[kh].start()
    par = parity()
    packed = jnp.concatenate([g_ref[s, 64:96, :].astype(F32) for s in range(16)], axis=0)
    ordered = exchange(packed, 16, 8).astype(BF)
    for h in range(2):
        full = dot(ordered, spread(h, par))
        back_ref[h] = jnp.where(same_block((512, 512)), full, 0.0).astype(BF)
    lane_k = (iota((128, 512), 1) >> 3) & 3
    mixed = []
    for kh in range(2):
        rows = [
            g_ref[source(p, g, kh, par), kh * 32 : kh * 32 + 32, :].astype(F32)
            for p in range(4)
            for g in range(4)
        ]
        turned = jnp.concatenate(rows, axis=0).T
        big = jnp.concatenate([jnp.where(lane_k == k, turned, 0.0) for k in range(4)], axis=0)
        copies[kh].wait()
        mixed.append(dot(x_ref[kh], big.astype(BF)).astype(BF))
    even = ((iota((mixed[0].shape[0], 128), 1) >> 5) & 1) == 0
    for p in range(4):
        lanes = slice(p * 128, (p + 1) * 128)
        a, b = mixed[0][:, lanes], mixed[1][:, lanes]
        out_ref[2 * p] = jnp.where(even, a, b)
        out_ref[2 * p + 1] = jnp.where(even, b, a)


def mix(x, gathered):
    rows = x.shape[0]
    return pl.pallas_call(
        mix_kernel,
        out_shape=(
            jax.ShapeDtypeStruct((8, rows, 128), BF),
            jax.ShapeDtypeStruct((2, 512, 512), BF),
        ),
        in_specs=[pl.BlockSpec(memory_space=pltpu.HBM), pl.BlockSpec()],
        scratch_shapes=[pltpu.VMEM((2, rows, 512), BF), pltpu.SemaphoreType.DMA((2,))],
        compiler_params=params(),
        cost_estimate=cost(rows * 1024 * 1024, 4 * rows * 1024),
        name="mix",
    )(in_hbm(x), gathered)


def middle_kernel(in_ref, back_ref, target_ref, student_ref, left_ref, out_ref):
    par = parity()
    total = jnp.zeros((512, 128), F32)
    turned = halves([in_ref[j] for j in range(8)])
    outs = []
    for h in range(2):
        lanes = slice(h * 512, (h + 1) * 512)
        v = dot(turned[h], back_ref[h], ((1,), (1,)))
        square = v * v
        p = 0.5 + 0.5 * jnp.tanh(v * (ROOT + (ROOT * CUBE) * square))
        act = v * p
        slope = p + (act - act * p) * (2.0 * ROOT + (6.0 * ROOT * CUBE) * square)
        student_ref[:, lanes] = act.astype(BF)
        grad = ((act - target_ref[:, lanes].astype(F32)) * slope).astype(BF)
        outs.append(dot(grad, back_ref[h]).astype(BF))
        full = dot(grad, turned[h], ((0,), (0,)))
        full = jnp.where(same_block((512, 512)), full, 0.0).astype(BF)
        total = total + dot(full, spread(h, par), ((1,), (1,)))
    low = iota((outs[0].shape[0], 128), 1) < 64
    for p in range(4):
        lanes = slice(p * 128, (p + 1) * 128)
        a, b = outs[0][:, lanes], outs[1][:, lanes]
        out_ref[2 * p] = jnp.where(low, a, b)
        out_ref[2 * p + 1] = jnp.where(low, b, a)
    ordered = exchange(total, 8, 16).astype(BF)
    for s in range(16):
        left_ref[s] = ordered[s * 32 : (s + 1) * 32, :]


def middle(received, back, target):
    rows = target.shape[0]
    return pl.pallas_call(
        middle_kernel,
        out_shape=(
            pltpu.VMEM((rows, 1024), BF),
            jax.ShapeDtypeStruct((16, 32, 128), BF),
            jax.ShapeDtypeStruct((8, rows, 128), BF),
        ),
        compiler_params=params(),
        cost_estimate=cost(2 * rows * 1024 * 1024, 10 * rows * 1024),
        name="middle",
    )(received, back, target)


def grads_kernel(student_ref, left_ref, back_ref, x_ref, student_hbm, out_ref, sem):
    copy = pltpu.make_async_copy(student_ref, student_hbm, sem)
    copy.start()
    par = parity()
    returned = split([back_ref[j] for j in range(8)])
    row_k = (iota((512, 128), 0) >> 3) & 3
    for kh in range(2):
        full = dot(returned[kh], x_ref[:, kh * 512 : (kh + 1) * 512], ((0,), (0,)))
        kept = jnp.zeros((512, 128), F32)
        for k in range(4):
            kept = jnp.where(row_k == k, full[:, k * 128 : (k + 1) * 128], kept)
        kept = kept.astype(BF)
        for p in range(4):
            for g in range(4):
                n = (p * 4 + g) * 32
                out_ref[source(p, g, kh, par), kh * 32 : kh * 32 + 32, :] = kept[n : n + 32, :]
    for s in range(16):
        out_ref[s, 64:96, :] = left_ref[s]
    copy.wait()


def grads(student, left, returned, x):
    rows = x.shape[0]
    return pl.pallas_call(
        grads_kernel,
        out_shape=(
            pltpu.HBM(student.shape, BF),
            jax.ShapeDtypeStruct((16, 96, 128), BF),
        ),
        out_specs=(pl.BlockSpec(memory_space=pltpu.HBM), pl.BlockSpec()),
        scratch_shapes=[pltpu.SemaphoreType.DMA],
        compiler_params=params(),
        cost_estimate=cost(2 * rows * 1024 * 1024, 8 * rows * 1024),
        name="grads",
    )(student, left, returned, x)


def sum_kernel(scale, in_ref, right_ref, left_ref):
    total = in_ref[0].astype(F32)
    for s in range(1, 16):
        total = total + in_ref[s].astype(F32)
    total = total * scale
    right_ref[...] = total[:64].reshape(8, 8, 128)
    left = total[64:]
    left_ref[:8] = left[:, :64].reshape(8, 4, 64)
    left_ref[8:] = left[:, 64:].reshape(8, 4, 64)


def sums(terms, scale):
    return pl.pallas_call(
        functools.partial(sum_kernel, scale),
        out_shape=(
            jax.ShapeDtypeStruct((8, 8, 128), F32),
            jax.ShapeDtypeStruct((16, 4, 64), F32),
        ),
        compiler_params=params(),
        name="sums",
    )(terms)


def shards(tokens, right_factor, left_factor, target):
    rows = tokens.shape[0]
    scale = 1.0 / math.sqrt(rows * lax.axis_size("seq"))
    gathered = lax.all_to_all(pack(right_factor, left_factor), "seq", 0, 0, tiled=True)
    mixed, back = mix(tokens, gathered)
    received = lax.all_to_all(mixed, "blk", 0, 0, tiled=True)
    student, left, out = middle(received, back, target)
    returned = lax.all_to_all(out, "blk", 0, 0, tiled=True)
    student, terms = grads(student, left, returned, tokens)
    terms = lax.all_to_all(terms, "seq", 0, 0, tiled=True)
    right_grad, left_grad = sums(terms, scale)
    return (student, right_grad, left_grad)


def solution(mesh):
    return jax.shard_map(
        shards,
        mesh=mesh,
        in_specs=(P("seq", "blk"), P("blk", "seq", None), P("blk", "seq", None), P("seq", "blk")),
        out_specs=(P("seq", "blk"), P("blk", "seq", None), P("blk", "seq", None)),
        check_vma=False,
    )
```

```python
import functools
import math

import jax
import jax.numpy as jnp
from jax import lax
from jax.experimental import pallas as pl
from jax.experimental.pallas import tpu as pltpu
from jax.sharding import PartitionSpec as P

BF = jnp.bfloat16
F32 = jnp.float32
MIB = 1 << 20
ROOT = math.sqrt(2.0 / math.pi)
CUBE = 0.044715


def iota(shape, dim):
    return lax.broadcasted_iota(jnp.int32, shape, dim)


def dot(a, b, dims=((1,), (0,))):
    return lax.dot_general(a, b, (dims, ((), ())), preferred_element_type=F32)


def params(limit=24):
    return pltpu.CompilerParams(vmem_limit_bytes=limit * MIB)


def cost(flops, size):
    return pl.CostEstimate(flops=int(flops), bytes_accessed=int(size), transcendentals=0)


def in_hbm(x):
    return pltpu.with_memory_space_constraint(x, pltpu.HBM)


def parity():
    return lax.rem(lax.axis_index("blk"), 2)


def joined(parts):
    return jnp.concatenate(parts, axis=1)


def halves(blocks):
    low = iota(blocks[0].shape, 1) < 64
    first = joined([jnp.where(low, blocks[2 * p], blocks[2 * p + 1]) for p in range(4)])
    second = joined([jnp.where(low, blocks[2 * p + 1], blocks[2 * p]) for p in range(4)])
    return first, second


def split(blocks):
    even = ((iota(blocks[0].shape, 1) >> 5) & 1) == 0
    first = joined([jnp.where(even, blocks[2 * p], blocks[2 * p + 1]) for p in range(4)])
    second = joined([jnp.where(even, blocks[2 * p + 1], blocks[2 * p]) for p in range(4)])
    return first, second


def chip(pair, g, kh):
    return 2 * pair + ((g & 1) ^ kh)


def core():
    return lax.rem(lax.axis_index("seq"), 2)


def flip():
    return lax.rem(lax.axis_index("seq") + lax.axis_index("blk"), 2)


def pack_kernel(right_hbm, left_hbm, out_ref, right_ref, left_ref, sems):
    copies = [
        pltpu.make_async_copy(right_hbm, right_ref, sems.at[0]),
        pltpu.make_async_copy(left_hbm, left_ref, sems.at[1]),
    ]
    for copy in copies:
        copy.start()
    for copy in copies:
        copy.wait()
    right = right_ref[...].astype(F32).reshape(64, 128)
    left = left_ref[...].astype(F32).reshape(64, 64)
    whole = jnp.concatenate([right, joined([left[:32], left[32:]])], axis=0).astype(BF)
    for s in range(8):
        out_ref[s] = whole


def pack(right, left):
    return pl.pallas_call(
        pack_kernel,
        in_specs=[pl.BlockSpec(memory_space=pltpu.HBM)] * 2,
        out_shape=jax.ShapeDtypeStruct((8, 96, 128), BF),
        scratch_shapes=[
            pltpu.VMEM(right.shape, BF),
            pltpu.VMEM(left.shape, BF),
            pltpu.SemaphoreType.DMA((2,)),
        ],
        compiler_params=params(),
        name="pack",
    )(in_hbm(right), in_hbm(left))


def exchange(x, a, b):
    low = iota((8, x.shape[1]), 0) < 4

    def tile(i, j):
        n = (i * b + j) * 4
        return x[n : n + 8]

    parts = []
    for j in range(0, b, 2):
        pairs = [(tile(i, j), tile(i + 1, j)) for i in range(0, a, 2)]
        parts += [jnp.where(low, u, pltpu.roll(v, 4, 0)) for u, v in pairs]
        parts += [jnp.where(low, pltpu.roll(u, 4, 0), v) for u, v in pairs]
    return jnp.concatenate(parts, axis=0)


def spread(h, par):
    r, f = iota((128, 512), 0), iota((128, 512), 1)
    device = ((f >> 7) << 1) + (((f >> 6) & 1) ^ h)
    k = (device << 3) + ((((f >> 5) & 1) ^ par) << 2) + ((f >> 3) & 3)
    return (r == k + h * 64).astype(F32).astype(BF)


def same_block(shape):
    return (iota(shape, 0) >> 6) == (iota(shape, 1) & 7)


def fetch_kernel(x_hbm, after_ref, out_ref, sem):
    copy = pltpu.make_async_copy(x_hbm, out_ref, sem)
    copy.start()
    copy.wait()


def fetch(x, after):
    return pl.pallas_call(
        fetch_kernel,
        in_specs=[pl.BlockSpec(memory_space=pltpu.HBM), pl.BlockSpec()],
        out_shape=pltpu.VMEM(x.shape, BF),
        scratch_shapes=[pltpu.SemaphoreType.DMA],
        compiler_params=params(8),
        cost_estimate=cost(0, 8 * MIB),
        name="fetch",
    )(in_hbm(x), after)


def mix_kernel(x_ref, own_ref, sib_ref, out_ref, back_ref):
    par = parity()
    first = core() == 0
    rows = []
    for n in range(8):
        own, sib = own_ref[n, 64:96, :].astype(F32), sib_ref[n, 64:96, :].astype(F32)
        rows += [jnp.where(first, own, sib), jnp.where(first, sib, own)]
    packed = jnp.concatenate(rows, axis=0)
    ordered = exchange(packed, 16, 8).astype(BF)
    for h in range(2):
        full = dot(ordered, spread(h, par))
        back_ref[h] = jnp.where(same_block((512, 512)), full, 0.0).astype(BF)
    lane_k = (iota((128, 512), 1) >> 3) & 3
    mixed = []
    for kh in range(2):
        rows = []
        for p in range(4):
            for g in range(4):
                place = (chip(p, g, kh), slice(kh * 32, kh * 32 + 32))
                own, sib = own_ref[place].astype(F32), sib_ref[place].astype(F32)
                rows.append(jnp.where(flip() == (g >> 1), own, sib))
        turned = jnp.concatenate(rows, axis=0).T
        big = jnp.concatenate([jnp.where(lane_k == k, turned, 0.0) for k in range(4)], axis=0)
        mixed.append(dot(x_ref[:, kh * 512 : (kh + 1) * 512], big.astype(BF)).astype(BF))
    even = ((iota((mixed[0].shape[0], 128), 1) >> 5) & 1) == 0
    for p in range(4):
        lanes = slice(p * 128, (p + 1) * 128)
        a, b = mixed[0][:, lanes], mixed[1][:, lanes]
        out_ref[2 * p] = jnp.where(even, a, b)
        out_ref[2 * p + 1] = jnp.where(even, b, a)


def mix(x, own, sibling):
    rows = x.shape[0]
    return pl.pallas_call(
        mix_kernel,
        out_shape=(
            jax.ShapeDtypeStruct((8, rows, 128), BF),
            jax.ShapeDtypeStruct((2, 512, 512), BF),
        ),
        compiler_params=params(),
        cost_estimate=cost(rows * 1024 * 1024, 4 * rows * 1024),
        name="mix",
    )(x, own, sibling)


def middle_kernel(in_ref, back_ref, target_ref, student_ref, left_ref, out_ref):
    par = parity()
    total = jnp.zeros((512, 128), F32)
    turned = halves([in_ref[j] for j in range(8)])
    outs = []
    for h in range(2):
        lanes = slice(h * 512, (h + 1) * 512)
        v = dot(turned[h], back_ref[h], ((1,), (1,)))
        square = v * v
        p = 0.5 + 0.5 * jnp.tanh(v * (ROOT + (ROOT * CUBE) * square))
        act = v * p
        slope = p + (act - act * p) * (2.0 * ROOT + (6.0 * ROOT * CUBE) * square)
        student_ref[:, lanes] = act.astype(BF)
        grad = ((act - target_ref[:, lanes].astype(F32)) * slope).astype(BF)
        outs.append(dot(grad, back_ref[h]).astype(BF))
        full = dot(grad, turned[h], ((0,), (0,)))
        full = jnp.where(same_block((512, 512)), full, 0.0).astype(BF)
        total = total + dot(full, spread(h, par), ((1,), (1,)))
    low = iota((outs[0].shape[0], 128), 1) < 64
    for p in range(4):
        lanes = slice(p * 128, (p + 1) * 128)
        a, b = outs[0][:, lanes], outs[1][:, lanes]
        out_ref[2 * p] = jnp.where(low, a, b)
        out_ref[2 * p + 1] = jnp.where(low, b, a)
    ordered = exchange(total, 8, 16)
    for s in range(16):
        left_ref[s] = ordered[s * 32 : (s + 1) * 32, :]


def middle(received, back, target):
    rows = target.shape[0]
    return pl.pallas_call(
        middle_kernel,
        out_shape=(
            pltpu.VMEM((rows, 1024), BF),
            jax.ShapeDtypeStruct((16, 32, 128), F32),
            jax.ShapeDtypeStruct((8, rows, 128), BF),
        ),
        compiler_params=params(),
        cost_estimate=cost(2 * rows * 1024 * 1024, 10 * rows * 1024),
        name="middle",
    )(received, back, target)


def grads_kernel(student_ref, left_ref, back_ref, x_ref, student_hbm, mine_ref, other_ref, sem):
    copy = pltpu.make_async_copy(student_ref, student_hbm, sem)
    copy.start()
    same = flip() == 0
    returned = split([back_ref[j] for j in range(8)])
    row_k = (iota((512, 128), 0) >> 3) & 3
    for kh in range(2):
        full = dot(returned[kh], x_ref[:, kh * 512 : (kh + 1) * 512], ((0,), (0,)))
        kept = jnp.zeros((512, 128), F32)
        for k in range(4):
            kept = jnp.where(row_k == k, full[:, k * 128 : (k + 1) * 128], kept)
        for p in range(4):
            for g in range(2):
                n = (p * 4 + g) * 32
                a, b = kept[n : n + 32], kept[n + 64 : n + 96]
                place = (chip(p, g, kh), slice(kh * 32, kh * 32 + 32))
                mine_ref[place] = jnp.where(same, a, b)
                other_ref[place] = jnp.where(same, b, a).astype(BF)
    for n in range(8):
        mine_ref[n, 64:96, :] = left_ref[2 * n + core()]
        other_ref[n, 64:96, :] = left_ref[2 * n + 1 - core()].astype(BF)
    copy.wait()


def grads(student, left, returned, x):
    rows = x.shape[0]
    return pl.pallas_call(
        grads_kernel,
        out_shape=(
            pltpu.HBM(student.shape, BF),
            jax.ShapeDtypeStruct((8, 96, 128), F32),
            jax.ShapeDtypeStruct((8, 96, 128), BF),
        ),
        out_specs=(pl.BlockSpec(memory_space=pltpu.HBM), pl.BlockSpec(), pl.BlockSpec()),
        scratch_shapes=[pltpu.SemaphoreType.DMA],
        compiler_params=params(),
        cost_estimate=cost(2 * rows * 1024 * 1024, 8 * rows * 1024),
        name="grads",
    )(student, left, returned, x)


def sum_kernel(scale, in_ref, right_ref, left_ref):
    total = in_ref[0].astype(F32)
    for s in range(1, 8):
        total = total + in_ref[s].astype(F32)
    total = total * scale
    right_ref[...] = total[:64].reshape(8, 8, 128)
    left = total[64:]
    left_ref[:8] = left[:, :64].reshape(8, 4, 64)
    left_ref[8:] = left[:, 64:].reshape(8, 4, 64)


def sums(terms, scale):
    return pl.pallas_call(
        functools.partial(sum_kernel, scale),
        out_shape=(
            jax.ShapeDtypeStruct((8, 8, 128), F32),
            jax.ShapeDtypeStruct((16, 4, 64), F32),
        ),
        compiler_params=params(),
        name="sums",
    )(terms)


def shards(tokens, right_factor, left_factor, target):
    rows = tokens.shape[0]
    scale = 1.0 / math.sqrt(rows * lax.axis_size("seq"))
    chips = [[2 * n + c for n in range(8)] for c in range(2)]
    across = [(n, n ^ 1) for n in range(16)]
    own = lax.all_to_all(
        pack(right_factor, left_factor), "seq", 0, 0, tiled=True, axis_index_groups=chips
    )
    mixed, back = mix(fetch(tokens, own), own, lax.ppermute(own, "seq", across))
    received = lax.all_to_all(mixed, "blk", 0, 0, tiled=True)
    student, left, out = middle(received, back, target)
    returned = lax.all_to_all(out, "blk", 0, 0, tiled=True)
    student, mine, other = grads(student, left, returned, tokens)
    terms = (mine + lax.ppermute(other, "seq", across).astype(F32)).astype(BF)
    terms = lax.all_to_all(terms, "seq", 0, 0, tiled=True, axis_index_groups=chips)
    right_grad, left_grad = sums(terms, scale)
    return (student, right_grad, left_grad)


def solution(mesh):
    return jax.shard_map(
        shards,
        mesh=mesh,
        in_specs=(P("seq", "blk"), P("blk", "seq", None), P("blk", "seq", None), P("seq", "blk")),
        out_specs=(P("seq", "blk"), P("blk", "seq", None), P("blk", "seq", None)),
        check_vma=False,
    )
```

```python
import functools
import math

import jax
import jax.numpy as jnp
from jax import lax
from jax.experimental import pallas as pl
from jax.experimental.pallas import tpu as pltpu
from jax.sharding import PartitionSpec as P

BF = jnp.bfloat16
F32 = jnp.float32
MIB = 1 << 20
ROOT = math.sqrt(2.0 / math.pi)
CUBE = 0.044715


def iota(shape, dim):
    return lax.broadcasted_iota(jnp.int32, shape, dim)


def dot(a, b, dims=((1,), (0,))):
    return lax.dot_general(a, b, (dims, ((), ())), preferred_element_type=F32)


def params(limit=24):
    return pltpu.CompilerParams(vmem_limit_bytes=limit * MIB)


def cost(flops, size):
    return pl.CostEstimate(flops=int(flops), bytes_accessed=int(size), transcendentals=0)


def in_hbm(x):
    return pltpu.with_memory_space_constraint(x, pltpu.HBM)


def parity():
    return lax.rem(lax.axis_index("blk"), 2)


def joined(parts):
    return jnp.concatenate(parts, axis=1)


def halves(blocks):
    low = iota(blocks[0].shape, 1) < 64
    first = joined([jnp.where(low, blocks[2 * p], blocks[2 * p + 1]) for p in range(4)])
    second = joined([jnp.where(low, blocks[2 * p + 1], blocks[2 * p]) for p in range(4)])
    return first, second


def split(blocks):
    even = ((iota(blocks[0].shape, 1) >> 5) & 1) == 0
    first = joined([jnp.where(even, blocks[2 * p], blocks[2 * p + 1]) for p in range(4)])
    second = joined([jnp.where(even, blocks[2 * p + 1], blocks[2 * p]) for p in range(4)])
    return first, second


def chip(pair, g, kh):
    return 2 * pair + ((g & 1) ^ kh)


def core():
    return lax.rem(lax.axis_index("seq"), 2)


def flip():
    return lax.rem(lax.axis_index("seq") + lax.axis_index("blk"), 2)


def pack_kernel(right_hbm, left_hbm, out_ref, right_ref, left_ref, sems):
    copies = [
        pltpu.make_async_copy(right_hbm, right_ref, sems.at[0]),
        pltpu.make_async_copy(left_hbm, left_ref, sems.at[1]),
    ]
    for copy in copies:
        copy.start()
    for copy in copies:
        copy.wait()
    right = right_ref[...].astype(F32).reshape(64, 128)
    left = left_ref[...].astype(F32).reshape(64, 64)
    whole = jnp.concatenate([right, joined([left[:32], left[32:]])], axis=0).astype(BF)
    out_ref[...] = whole


def pack(right, left):
    return pl.pallas_call(
        pack_kernel,
        in_specs=[pl.BlockSpec(memory_space=pltpu.HBM)] * 2,
        out_shape=jax.ShapeDtypeStruct((96, 128), BF),
        scratch_shapes=[
            pltpu.VMEM(right.shape, BF),
            pltpu.VMEM(left.shape, BF),
            pltpu.SemaphoreType.DMA((2,)),
        ],
        compiler_params=params(),
        name="pack",
    )(in_hbm(right), in_hbm(left))


def pair_kernel(own_ref, sib_ref, after_ref, out_ref):
    first = core() == 0
    own, sib = own_ref[...].astype(F32), sib_ref[...].astype(F32)
    low, high = jnp.where(first, own, sib).astype(BF), jnp.where(first, sib, own).astype(BF)
    for n in range(8):
        out_ref[n, 0:96, :] = low
        out_ref[n, 96:192, :] = high


def pair(own, sibling, after):
    return pl.pallas_call(
        pair_kernel,
        in_specs=[pl.BlockSpec(), pl.BlockSpec(), pl.BlockSpec(memory_space=pl.ANY)],
        out_shape=jax.ShapeDtypeStruct((8, 192, 128), BF),
        compiler_params=params(8),
        name="pair",
    )(own, sibling, after)


def plane():
    return lax.rem(lax.div(lax.axis_index("seq"), 2), 2)


def other_kernel(g_ref, out_ref):
    there = 1 - plane()
    for z in range(4):
        out_ref[z] = g_ref[2 * z + there]


def other_half(gathered):
    return pl.pallas_call(
        other_kernel,
        out_shape=jax.ShapeDtypeStruct((4, 192, 128), BF),
        compiler_params=params(8),
        name="other_half",
    )(gathered)


def pass_kernel(x_ref, turn_ref, out_ref):
    pass


def pass_on(x, turn):
    return pl.pallas_call(
        pass_kernel,
        out_shape=jax.ShapeDtypeStruct(x.shape, x.dtype),
        in_specs=[pl.BlockSpec(memory_space=pl.ANY)] * 2,
        out_specs=pl.BlockSpec(memory_space=pl.ANY),
        input_output_aliases={0: 0},
        compiler_params=params(8),
        name="pass_on",
    )(x, turn)


def exchange(x, a, b):
    low = iota((8, x.shape[1]), 0) < 4

    def tile(i, j):
        n = (i * b + j) * 4
        return x[n : n + 8]

    parts = []
    for j in range(0, b, 2):
        pairs = [(tile(i, j), tile(i + 1, j)) for i in range(0, a, 2)]
        parts += [jnp.where(low, u, pltpu.roll(v, 4, 0)) for u, v in pairs]
        parts += [jnp.where(low, pltpu.roll(u, 4, 0), v) for u, v in pairs]
    return jnp.concatenate(parts, axis=0)


def spread(h, par):
    r, f = iota((128, 512), 0), iota((128, 512), 1)
    device = ((f >> 7) << 1) + (((f >> 6) & 1) ^ h)
    k = (device << 3) + ((((f >> 5) & 1) ^ par) << 2) + ((f >> 3) & 3)
    return (r == k + h * 64).astype(F32).astype(BF)


def same_block(shape):
    return (iota(shape, 0) >> 6) == (iota(shape, 1) & 7)


def fetch_kernel(x_hbm, after_ref, out_ref, sem):
    copy = pltpu.make_async_copy(x_hbm, out_ref, sem)
    copy.start()
    copy.wait()


def fetch(x, after):
    return pl.pallas_call(
        fetch_kernel,
        in_specs=[pl.BlockSpec(memory_space=pltpu.HBM), pl.BlockSpec()],
        out_shape=pltpu.VMEM(x.shape, BF),
        scratch_shapes=[pltpu.SemaphoreType.DMA],
        compiler_params=params(8),
        cost_estimate=cost(0, 8 * MIB),
        name="fetch",
    )(in_hbm(x), after)


def mix_kernel(x_ref, all_ref, near_ref, far_ref, out_ref, back_ref, g_ref):
    @pl.when(core() == 0)
    def _():
        g_ref[...] = all_ref[...]

    @pl.when(core() == 1)
    def _():
        here = plane()
        for z in range(4):
            g_ref[2 * z + here] = near_ref[z]
            g_ref[2 * z + 1 - here] = far_ref[z]

    par = parity()
    packed = jnp.concatenate(
        [g_ref[n, c * 96 + 64 : c * 96 + 96, :].astype(F32) for n in range(8) for c in range(2)],
        axis=0,
    )
    ordered = exchange(packed, 16, 8).astype(BF)
    for h in range(2):
        full = dot(ordered, spread(h, par))
        back_ref[h] = jnp.where(same_block((512, 512)), full, 0.0).astype(BF)
    lane_k = (iota((128, 512), 1) >> 3) & 3
    mixed = []
    for kh in range(2):
        rows = []
        for p in range(4):
            for g in range(4):
                n, k = chip(p, g, kh), kh * 32
                low, high = g_ref[n, k : k + 32, :], g_ref[n, k + 96 : k + 128, :]
                rows.append(jnp.where(par == (g >> 1), low.astype(F32), high.astype(F32)))
        turned = jnp.concatenate(rows, axis=0).T
        big = jnp.concatenate([jnp.where(lane_k == k, turned, 0.0) for k in range(4)], axis=0)
        mixed.append(dot(x_ref[:, kh * 512 : (kh + 1) * 512], big.astype(BF)).astype(BF))
    even = ((iota((mixed[0].shape[0], 128), 1) >> 5) & 1) == 0
    for p in range(4):
        lanes = slice(p * 128, (p + 1) * 128)
        a, b = mixed[0][:, lanes], mixed[1][:, lanes]
        out_ref[2 * p] = jnp.where(even, a, b)
        out_ref[2 * p + 1] = jnp.where(even, b, a)


def mix(x, gathered, near, far):
    rows = x.shape[0]
    return pl.pallas_call(
        mix_kernel,
        out_shape=(
            jax.ShapeDtypeStruct((8, rows, 128), BF),
            jax.ShapeDtypeStruct((2, 512, 512), BF),
        ),
        scratch_shapes=[pltpu.VMEM((8, 192, 128), BF)],
        compiler_params=params(),
        cost_estimate=cost(rows * 1024 * 1024, 4 * rows * 1024),
        name="mix",
    )(x, gathered, near, far)


def middle_kernel(in_ref, back_ref, target_ref, student_ref, left_ref, out_ref):
    par = parity()
    total = jnp.zeros((512, 128), F32)
    turned = halves([in_ref[j] for j in range(8)])
    outs = []
    for h in range(2):
        lanes = slice(h * 512, (h + 1) * 512)
        v = dot(turned[h], back_ref[h], ((1,), (1,)))
        square = v * v
        p = 0.5 + 0.5 * jnp.tanh(v * (ROOT + (ROOT * CUBE) * square))
        act = v * p
        slope = p + (act - act * p) * (2.0 * ROOT + (6.0 * ROOT * CUBE) * square)
        student_ref[:, lanes] = act.astype(BF)
        grad = ((act - target_ref[:, lanes].astype(F32)) * slope).astype(BF)
        outs.append(dot(grad, back_ref[h]).astype(BF))
        full = dot(grad, turned[h], ((0,), (0,)))
        full = jnp.where(same_block((512, 512)), full, 0.0).astype(BF)
        total = total + dot(full, spread(h, par), ((1,), (1,)))
    low = iota((outs[0].shape[0], 128), 1) < 64
    for p in range(4):
        lanes = slice(p * 128, (p + 1) * 128)
        a, b = outs[0][:, lanes], outs[1][:, lanes]
        out_ref[2 * p] = jnp.where(low, a, b)
        out_ref[2 * p + 1] = jnp.where(low, b, a)
    ordered = exchange(total, 8, 16)
    for s in range(16):
        left_ref[s] = ordered[s * 32 : (s + 1) * 32, :]


def middle(received, back, target):
    rows = target.shape[0]
    return pl.pallas_call(
        middle_kernel,
        out_shape=(
            pltpu.VMEM((rows, 1024), BF),
            jax.ShapeDtypeStruct((16, 32, 128), F32),
            jax.ShapeDtypeStruct((8, rows, 128), BF),
        ),
        compiler_params=params(),
        cost_estimate=cost(2 * rows * 1024 * 1024, 10 * rows * 1024),
        name="middle",
    )(received, back, target)


def grads_kernel(student_ref, left_ref, back_ref, x_ref, student_hbm, mine_ref, other_ref, sem):
    copy = pltpu.make_async_copy(student_ref, student_hbm, sem)
    copy.start()
    same = flip() == 0
    returned = split([back_ref[j] for j in range(8)])
    row_k = (iota((512, 128), 0) >> 3) & 3
    for kh in range(2):
        full = dot(returned[kh], x_ref[:, kh * 512 : (kh + 1) * 512], ((0,), (0,)))
        kept = jnp.zeros((512, 128), F32)
        for k in range(4):
            kept = jnp.where(row_k == k, full[:, k * 128 : (k + 1) * 128], kept)
        for p in range(4):
            for g in range(2):
                n = (p * 4 + g) * 32
                a, b = kept[n : n + 32], kept[n + 64 : n + 96]
                place = (chip(p, g, kh), slice(kh * 32, kh * 32 + 32))
                mine_ref[place] = jnp.where(same, a, b)
                other_ref[place] = jnp.where(same, b, a).astype(BF)
    for n in range(8):
        mine_ref[n, 64:96, :] = left_ref[2 * n + core()]
        other_ref[n, 64:96, :] = left_ref[2 * n + 1 - core()].astype(BF)
    copy.wait()


def grads(student, left, returned, x):
    rows = x.shape[0]
    return pl.pallas_call(
        grads_kernel,
        out_shape=(
            pltpu.HBM(student.shape, BF),
            jax.ShapeDtypeStruct((8, 96, 128), F32),
            jax.ShapeDtypeStruct((8, 96, 128), BF),
        ),
        out_specs=(pl.BlockSpec(memory_space=pltpu.HBM), pl.BlockSpec(), pl.BlockSpec()),
        scratch_shapes=[pltpu.SemaphoreType.DMA],
        compiler_params=params(),
        cost_estimate=cost(2 * rows * 1024 * 1024, 8 * rows * 1024),
        name="grads",
    )(student, left, returned, x)


def sum_kernel(scale, in_ref, right_ref, left_ref):
    total = in_ref[0].astype(F32)
    for s in range(1, 8):
        total = total + in_ref[s].astype(F32)
    total = total * scale
    right_ref[...] = total[:64].reshape(8, 8, 128)
    left = total[64:]
    left_ref[:8] = left[:, :64].reshape(8, 4, 64)
    left_ref[8:] = left[:, 64:].reshape(8, 4, 64)


def sums(terms, scale):
    return pl.pallas_call(
        functools.partial(sum_kernel, scale),
        out_shape=(
            jax.ShapeDtypeStruct((8, 8, 128), F32),
            jax.ShapeDtypeStruct((16, 4, 64), F32),
        ),
        compiler_params=params(),
        name="sums",
    )(terms)


def shards(tokens, right_factor, left_factor, target):
    rows = tokens.shape[0]
    scale = 1.0 / math.sqrt(rows * lax.axis_size("seq"))
    chips = [[2 * n + c for n in range(8)] for c in range(2)]
    across = [(n, n ^ 1) for n in range(16)]
    own = pack(right_factor, left_factor)
    x = fetch(tokens, own)
    share = pair(own, lax.ppermute(own, "seq", across), x)

    def gather(share):
        return lax.all_to_all(share, "seq", 0, 0, tiled=True, axis_index_groups=chips)

    def gather_z(share):
        lines = [[4 * z + n for z in range(4)] for n in range(4)]
        return lax.all_to_all(share, "seq", 0, 0, tiled=True, axis_index_groups=lines)

    first = lax.axis_index("seq") % 2 == 0
    gathered = lax.cond(first, gather, lambda share: share, share)
    far = lax.ppermute(other_half(gathered), "seq", [(2 * n, 2 * n + 1) for n in range(8)])
    near = lax.cond(first, lambda share: share, gather_z, pass_on(share[:4], far))
    mixed, back = mix(x, gathered, near, far)
    received = lax.all_to_all(mixed, "blk", 0, 0, tiled=True)
    student, left, out = middle(received, back, target)
    returned = lax.all_to_all(out, "blk", 0, 0, tiled=True)
    student, mine, other = grads(student, left, returned, x)
    terms = (mine + lax.ppermute(other, "seq", across).astype(F32)).astype(BF)
    terms = lax.all_to_all(terms, "seq", 0, 0, tiled=True, axis_index_groups=chips)
    right_grad, left_grad = sums(terms, scale)
    return (student, right_grad, left_grad)


def solution(mesh):
    return jax.shard_map(
        shards,
        mesh=mesh,
        in_specs=(P("seq", "blk"), P("blk", "seq", None), P("blk", "seq", None), P("seq", "blk")),
        out_specs=(P("seq", "blk"), P("blk", "seq", None), P("blk", "seq", None)),
        check_vma=False,
    )
```

```python
import functools
import math

import jax
import jax.numpy as jnp
from jax import lax
from jax.experimental import pallas as pl
from jax.experimental.pallas import tpu as pltpu
from jax.sharding import PartitionSpec as P

BF = jnp.bfloat16
F32 = jnp.float32
MIB = 1 << 20
ROOT = math.sqrt(2.0 / math.pi)
CUBE = 0.044715


def iota(shape, dim):
    return lax.broadcasted_iota(jnp.int32, shape, dim)


def dot(a, b, dims=((1,), (0,))):
    return lax.dot_general(a, b, (dims, ((), ())), preferred_element_type=F32)


def params(limit=24):
    return pltpu.CompilerParams(vmem_limit_bytes=limit * MIB)


def cost(flops, size):
    return pl.CostEstimate(flops=int(flops), bytes_accessed=int(size), transcendentals=0)


def in_hbm(x):
    return pltpu.with_memory_space_constraint(x, pltpu.HBM)


def parity():
    return lax.rem(lax.axis_index("blk"), 2)


def joined(parts):
    return jnp.concatenate(parts, axis=1)


def halves(blocks):
    low = iota(blocks[0].shape, 1) < 64
    first = joined([jnp.where(low, blocks[2 * p], blocks[2 * p + 1]) for p in range(4)])
    second = joined([jnp.where(low, blocks[2 * p + 1], blocks[2 * p]) for p in range(4)])
    return first, second


def split(blocks):
    even = ((iota(blocks[0].shape, 1) >> 5) & 1) == 0
    first = joined([jnp.where(even, blocks[2 * p], blocks[2 * p + 1]) for p in range(4)])
    second = joined([jnp.where(even, blocks[2 * p + 1], blocks[2 * p]) for p in range(4)])
    return first, second


def chip(pair, g, kh):
    return 2 * pair + ((g & 1) ^ kh)


def core():
    return lax.rem(lax.axis_index("seq"), 2)


def flip():
    return lax.rem(lax.axis_index("seq") + lax.axis_index("blk"), 2)


def pack_kernel(right_hbm, left_hbm, out_ref, right_ref, left_ref, sems):
    copies = [
        pltpu.make_async_copy(right_hbm, right_ref, sems.at[0]),
        pltpu.make_async_copy(left_hbm, left_ref, sems.at[1]),
    ]
    for copy in copies:
        copy.start()
    for copy in copies:
        copy.wait()
    right = right_ref[...].astype(F32).reshape(64, 128)
    left = left_ref[...].astype(F32).reshape(64, 64)
    whole = jnp.concatenate([right, joined([left[:32], left[32:]])], axis=0).astype(BF)
    out_ref[...] = whole


def pack(right, left):
    return pl.pallas_call(
        pack_kernel,
        in_specs=[pl.BlockSpec(memory_space=pltpu.HBM)] * 2,
        out_shape=jax.ShapeDtypeStruct((96, 128), BF),
        scratch_shapes=[
            pltpu.VMEM(right.shape, BF),
            pltpu.VMEM(left.shape, BF),
            pltpu.SemaphoreType.DMA((2,)),
        ],
        compiler_params=params(),
        name="pack",
    )(in_hbm(right), in_hbm(left))


def pair_kernel(own_ref, sib_ref, after_ref, out_ref):
    first = core() == 0
    own, sib = own_ref[...].astype(F32), sib_ref[...].astype(F32)
    low, high = jnp.where(first, own, sib).astype(BF), jnp.where(first, sib, own).astype(BF)
    for n in range(8):
        out_ref[n, 0:96, :] = low
        out_ref[n, 96:192, :] = high


def pair(own, sibling, after):
    return pl.pallas_call(
        pair_kernel,
        in_specs=[pl.BlockSpec(), pl.BlockSpec(), pl.BlockSpec(memory_space=pl.ANY)],
        out_shape=jax.ShapeDtypeStruct((8, 192, 128), BF),
        compiler_params=params(8),
        name="pair",
    )(own, sibling, after)


def plane():
    return lax.rem(lax.div(lax.axis_index("seq"), 2), 2)


def other_kernel(g_ref, out_ref):
    there = 1 - plane()
    for z in range(4):
        out_ref[z] = g_ref[2 * z + there]


def other_half(gathered):
    return pl.pallas_call(
        other_kernel,
        out_shape=jax.ShapeDtypeStruct((4, 192, 128), BF),
        compiler_params=params(8),
        name="other_half",
    )(gathered)


def pass_kernel(x_ref, turn_ref, out_ref):
    pass


def pass_on(x, turn):
    return pl.pallas_call(
        pass_kernel,
        out_shape=jax.ShapeDtypeStruct(x.shape, x.dtype),
        in_specs=[pl.BlockSpec(memory_space=pl.ANY)] * 2,
        out_specs=pl.BlockSpec(memory_space=pl.ANY),
        input_output_aliases={0: 0},
        compiler_params=params(8),
        name="pass_on",
    )(x, turn)


def exchange(x, a, b):
    low = iota((8, x.shape[1]), 0) < 4

    def tile(i, j):
        n = (i * b + j) * 4
        return x[n : n + 8]

    parts = []
    for j in range(0, b, 2):
        pairs = [(tile(i, j), tile(i + 1, j)) for i in range(0, a, 2)]
        parts += [jnp.where(low, u, pltpu.roll(v, 4, 0)) for u, v in pairs]
        parts += [jnp.where(low, pltpu.roll(u, 4, 0), v) for u, v in pairs]
    return jnp.concatenate(parts, axis=0)


def spread(h, par):
    r, f = iota((128, 512), 0), iota((128, 512), 1)
    device = ((f >> 7) << 1) + (((f >> 6) & 1) ^ h)
    k = (device << 3) + ((((f >> 5) & 1) ^ par) << 2) + ((f >> 3) & 3)
    return (r == k + h * 64).astype(F32).astype(BF)


def same_block(shape):
    return (iota(shape, 0) >> 6) == (iota(shape, 1) & 7)


def fetch_kernel(x_hbm, after_ref, out_ref, sem):
    @pl.when(core() == 0)
    def _():
        copy = pltpu.make_async_copy(x_hbm, out_ref, sem)
        copy.start()
        copy.wait()


def fetch(x, after):
    return pl.pallas_call(
        fetch_kernel,
        in_specs=[pl.BlockSpec(memory_space=pltpu.HBM), pl.BlockSpec()],
        out_shape=pltpu.VMEM(x.shape, BF),
        scratch_shapes=[pltpu.SemaphoreType.DMA],
        compiler_params=params(8),
        cost_estimate=cost(0, 8 * MIB),
        name="fetch",
    )(in_hbm(x), after)


def mix_body(x_ref, g_ref, out_ref, back_ref):
    par = parity()
    packed = jnp.concatenate(
        [g_ref[n, c * 96 + 64 : c * 96 + 96, :].astype(F32) for n in range(8) for c in range(2)],
        axis=0,
    )
    ordered = exchange(packed, 16, 8).astype(BF)
    for h in range(2):
        full = dot(ordered, spread(h, par))
        back_ref[h] = jnp.where(same_block((512, 512)), full, 0.0).astype(BF)
    lane_k = (iota((128, 512), 1) >> 3) & 3
    mixed = []
    for kh in range(2):
        rows = []
        for p in range(4):
            for g in range(4):
                n, k = chip(p, g, kh), kh * 32
                low, high = g_ref[n, k : k + 32, :], g_ref[n, k + 96 : k + 128, :]
                rows.append(jnp.where(par == (g >> 1), low.astype(F32), high.astype(F32)))
        turned = jnp.concatenate(rows, axis=0).T
        big = jnp.concatenate([jnp.where(lane_k == k, turned, 0.0) for k in range(4)], axis=0)
        mixed.append(dot(x_ref[:, kh * 512 : (kh + 1) * 512], big.astype(BF)).astype(BF))
    even = ((iota((mixed[0].shape[0], 128), 1) >> 5) & 1) == 0
    for p in range(4):
        lanes = slice(p * 128, (p + 1) * 128)
        a, b = mixed[0][:, lanes], mixed[1][:, lanes]
        out_ref[2 * p] = jnp.where(even, a, b)
        out_ref[2 * p + 1] = jnp.where(even, b, a)


def mix_kernel(x_hbm, x_ref, all_ref, near_ref, far_ref, out_ref, back_ref, g_ref, late_ref, sem):
    @pl.when(core() == 0)
    def _():
        mix_body(x_ref, all_ref, out_ref, back_ref)

    @pl.when(core() == 1)
    def _():
        copy = pltpu.make_async_copy(x_hbm, late_ref, sem)
        copy.start()
        here = plane()
        for z in range(4):
            g_ref[2 * z + here] = near_ref[z]
            g_ref[2 * z + 1 - here] = far_ref[z]
        copy.wait()
        mix_body(late_ref, g_ref, out_ref, back_ref)


def mix(tokens, x, gathered, near, far):
    rows = x.shape[0]
    return pl.pallas_call(
        mix_kernel,
        out_shape=(
            jax.ShapeDtypeStruct((8, rows, 128), BF),
            jax.ShapeDtypeStruct((2, 512, 512), BF),
        ),
        in_specs=[pl.BlockSpec(memory_space=pltpu.HBM)] + [pl.BlockSpec()] * 4,
        scratch_shapes=[
            pltpu.VMEM((8, 192, 128), BF),
            pltpu.VMEM(x.shape, BF),
            pltpu.SemaphoreType.DMA,
        ],
        compiler_params=params(),
        cost_estimate=cost(rows * 1024 * 1024, 4 * rows * 1024),
        name="mix",
    )(in_hbm(tokens), x, gathered, near, far)


def middle_kernel(in_ref, back_ref, target_ref, student_ref, left_ref, out_ref):
    par = parity()
    total = jnp.zeros((512, 128), F32)
    turned = halves([in_ref[j] for j in range(8)])
    outs = []
    for h in range(2):
        lanes = slice(h * 512, (h + 1) * 512)
        v = dot(turned[h], back_ref[h], ((1,), (1,)))
        square = v * v
        p = 0.5 + 0.5 * jnp.tanh(v * (ROOT + (ROOT * CUBE) * square))
        act = v * p
        slope = p + (act - act * p) * (2.0 * ROOT + (6.0 * ROOT * CUBE) * square)
        student_ref[:, lanes] = act.astype(BF)
        grad = ((act - target_ref[:, lanes].astype(F32)) * slope).astype(BF)
        outs.append(dot(grad, back_ref[h]).astype(BF))
        full = dot(grad, turned[h], ((0,), (0,)))
        full = jnp.where(same_block((512, 512)), full, 0.0).astype(BF)
        total = total + dot(full, spread(h, par), ((1,), (1,)))
    low = iota((outs[0].shape[0], 128), 1) < 64
    for p in range(4):
        lanes = slice(p * 128, (p + 1) * 128)
        a, b = outs[0][:, lanes], outs[1][:, lanes]
        out_ref[2 * p] = jnp.where(low, a, b)
        out_ref[2 * p + 1] = jnp.where(low, b, a)
    ordered = exchange(total, 8, 16)
    for s in range(16):
        left_ref[s] = ordered[s * 32 : (s + 1) * 32, :]


def middle(received, back, target):
    rows = target.shape[0]
    return pl.pallas_call(
        middle_kernel,
        out_shape=(
            pltpu.VMEM((rows, 1024), BF),
            jax.ShapeDtypeStruct((16, 32, 128), F32),
            jax.ShapeDtypeStruct((8, rows, 128), BF),
        ),
        compiler_params=params(),
        cost_estimate=cost(2 * rows * 1024 * 1024, 10 * rows * 1024),
        name="middle",
    )(received, back, target)


def grads_kernel(student_ref, left_ref, back_ref, x_ref, student_hbm, mine_ref, other_ref, sem):
    copy = pltpu.make_async_copy(student_ref, student_hbm, sem)
    copy.start()
    same = flip() == 0
    returned = split([back_ref[j] for j in range(8)])
    row_k = (iota((512, 128), 0) >> 3) & 3
    for kh in range(2):
        full = dot(returned[kh], x_ref[:, kh * 512 : (kh + 1) * 512], ((0,), (0,)))
        kept = jnp.zeros((512, 128), F32)
        for k in range(4):
            kept = jnp.where(row_k == k, full[:, k * 128 : (k + 1) * 128], kept)
        for p in range(4):
            for g in range(2):
                n = (p * 4 + g) * 32
                a, b = kept[n : n + 32], kept[n + 64 : n + 96]
                place = (chip(p, g, kh), slice(kh * 32, kh * 32 + 32))
                mine_ref[place] = jnp.where(same, a, b)
                other_ref[place] = jnp.where(same, b, a).astype(BF)
    for n in range(8):
        mine_ref[n, 64:96, :] = left_ref[2 * n + core()]
        other_ref[n, 64:96, :] = left_ref[2 * n + 1 - core()].astype(BF)
    copy.wait()


def grads(student, left, returned, x):
    rows = x.shape[0]
    return pl.pallas_call(
        grads_kernel,
        out_shape=(
            pltpu.HBM(student.shape, BF),
            jax.ShapeDtypeStruct((8, 96, 128), F32),
            jax.ShapeDtypeStruct((8, 96, 128), BF),
        ),
        out_specs=(pl.BlockSpec(memory_space=pltpu.HBM), pl.BlockSpec(), pl.BlockSpec()),
        scratch_shapes=[pltpu.SemaphoreType.DMA],
        compiler_params=params(),
        cost_estimate=cost(2 * rows * 1024 * 1024, 8 * rows * 1024),
        name="grads",
    )(student, left, returned, x)


def sum_kernel(scale, in_ref, right_ref, left_ref):
    total = in_ref[0].astype(F32)
    for s in range(1, 8):
        total = total + in_ref[s].astype(F32)
    total = total * scale
    right_ref[...] = total[:64].reshape(8, 8, 128)
    left = total[64:]
    left_ref[:8] = left[:, :64].reshape(8, 4, 64)
    left_ref[8:] = left[:, 64:].reshape(8, 4, 64)


def sums(terms, scale):
    return pl.pallas_call(
        functools.partial(sum_kernel, scale),
        out_shape=(
            jax.ShapeDtypeStruct((8, 8, 128), F32),
            jax.ShapeDtypeStruct((16, 4, 64), F32),
        ),
        compiler_params=params(),
        name="sums",
    )(terms)


def shards(tokens, right_factor, left_factor, target):
    rows = tokens.shape[0]
    scale = 1.0 / math.sqrt(rows * lax.axis_size("seq"))
    chips = [[2 * n + c for n in range(8)] for c in range(2)]
    across = [(n, n ^ 1) for n in range(16)]
    own = pack(right_factor, left_factor)
    x = fetch(tokens, own)
    share = pair(own, lax.ppermute(own, "seq", across), x)

    def gather(share):
        return lax.all_to_all(share, "seq", 0, 0, tiled=True, axis_index_groups=chips)

    def gather_z(share):
        lines = [[4 * z + n for z in range(4)] for n in range(4)]
        return lax.all_to_all(share, "seq", 0, 0, tiled=True, axis_index_groups=lines)

    first = lax.axis_index("seq") % 2 == 0
    gathered = lax.cond(first, gather, lambda share: share, share)
    far = lax.ppermute(other_half(gathered), "seq", [(2 * n, 2 * n + 1) for n in range(8)])
    near = lax.cond(first, lambda share: share, gather_z, pass_on(share[:4], far))
    mixed, back = mix(tokens, x, gathered, near, far)
    received = lax.all_to_all(mixed, "blk", 0, 0, tiled=True)
    student, left, out = middle(received, back, target)
    returned = lax.all_to_all(out, "blk", 0, 0, tiled=True)
    student, mine, other = grads(student, left, returned, tokens)
    terms = (mine + lax.ppermute(other, "seq", across).astype(F32)).astype(BF)
    terms = lax.all_to_all(terms, "seq", 0, 0, tiled=True, axis_index_groups=chips)
    right_grad, left_grad = sums(terms, scale)
    return (student, right_grad, left_grad)


def solution(mesh):
    return jax.shard_map(
        shards,
        mesh=mesh,
        in_specs=(P("seq", "blk"), P("blk", "seq", None), P("blk", "seq", None), P("seq", "blk")),
        out_specs=(P("seq", "blk"), P("blk", "seq", None), P("blk", "seq", None)),
        check_vma=False,
    )
```

```python
import functools
import math

import jax
import jax.numpy as jnp
from jax import lax
from jax.experimental import pallas as pl
from jax.experimental.pallas import tpu as pltpu
from jax.sharding import PartitionSpec as P

BF = jnp.bfloat16
F32 = jnp.float32
MIB = 1 << 20
ROOT = math.sqrt(2.0 / math.pi)
CUBE = 0.044715


def iota(shape, dim):
    return lax.broadcasted_iota(jnp.int32, shape, dim)


def dot(a, b, dims=((1,), (0,))):
    return lax.dot_general(a, b, (dims, ((), ())), preferred_element_type=F32)


def params(limit=24):
    return pltpu.CompilerParams(vmem_limit_bytes=limit * MIB)


def cost(flops, size):
    return pl.CostEstimate(flops=int(flops), bytes_accessed=int(size), transcendentals=0)


def in_hbm(x):
    return pltpu.with_memory_space_constraint(x, pltpu.HBM)


def parity():
    return lax.rem(lax.axis_index("blk"), 2)


def joined(parts):
    return jnp.concatenate(parts, axis=1)


def halves(blocks):
    low = iota(blocks[0].shape, 1) < 64
    first = joined([jnp.where(low, blocks[2 * p], blocks[2 * p + 1]) for p in range(4)])
    second = joined([jnp.where(low, blocks[2 * p + 1], blocks[2 * p]) for p in range(4)])
    return first, second


def split(blocks):
    even = ((iota(blocks[0].shape, 1) >> 5) & 1) == 0
    first = joined([jnp.where(even, blocks[2 * p], blocks[2 * p + 1]) for p in range(4)])
    second = joined([jnp.where(even, blocks[2 * p + 1], blocks[2 * p]) for p in range(4)])
    return first, second


def chip(pair, g, kh):
    return 2 * pair + ((g & 1) ^ kh)


def core():
    return lax.rem(lax.axis_index("seq"), 2)


def flip():
    return lax.rem(lax.axis_index("seq") + lax.axis_index("blk"), 2)


def pack_kernel(right_hbm, left_hbm, out_ref, right_ref, left_ref, sems):
    copies = [
        pltpu.make_async_copy(right_hbm, right_ref, sems.at[0]),
        pltpu.make_async_copy(left_hbm, left_ref, sems.at[1]),
    ]
    for copy in copies:
        copy.start()
    for copy in copies:
        copy.wait()
    right = right_ref[...].astype(F32).reshape(64, 128)
    left = left_ref[...].astype(F32).reshape(64, 64)
    whole = jnp.concatenate([right, joined([left[:32], left[32:]])], axis=0).astype(BF)
    out_ref[...] = whole


def pack(right, left):
    return pl.pallas_call(
        pack_kernel,
        in_specs=[pl.BlockSpec(memory_space=pltpu.HBM)] * 2,
        out_shape=jax.ShapeDtypeStruct((96, 128), BF),
        scratch_shapes=[
            pltpu.VMEM(right.shape, BF),
            pltpu.VMEM(left.shape, BF),
            pltpu.SemaphoreType.DMA((2,)),
        ],
        compiler_params=params(),
        name="pack",
    )(in_hbm(right), in_hbm(left))


def pair_kernel(own_ref, sib_ref, after_ref, out_ref):
    first = core() == 0
    own, sib = own_ref[...].astype(F32), sib_ref[...].astype(F32)
    low, high = jnp.where(first, own, sib).astype(BF), jnp.where(first, sib, own).astype(BF)
    for n in range(8):
        out_ref[n, 0:96, :] = low
        out_ref[n, 96:192, :] = high


def pair(own, sibling, after):
    return pl.pallas_call(
        pair_kernel,
        in_specs=[pl.BlockSpec(), pl.BlockSpec(), pl.BlockSpec(memory_space=pl.ANY)],
        out_shape=jax.ShapeDtypeStruct((8, 192, 128), BF),
        compiler_params=params(8),
        name="pair",
    )(own, sibling, after)


def plane():
    return lax.rem(lax.div(lax.axis_index("seq"), 2), 2)


def other_kernel(g_ref, out_ref):
    there = 1 - plane()
    for z in range(4):
        out_ref[z] = g_ref[2 * z + there]


def other_half(gathered):
    return pl.pallas_call(
        other_kernel,
        out_shape=jax.ShapeDtypeStruct((4, 192, 128), BF),
        compiler_params=params(8),
        name="other_half",
    )(gathered)


def pass_kernel(x_ref, turn_ref, out_ref):
    pass


def pass_on(x, turn):
    return pl.pallas_call(
        pass_kernel,
        out_shape=jax.ShapeDtypeStruct(x.shape, x.dtype),
        in_specs=[pl.BlockSpec(memory_space=pl.ANY)] * 2,
        out_specs=pl.BlockSpec(memory_space=pl.ANY),
        input_output_aliases={0: 0},
        compiler_params=params(8),
        name="pass_on",
    )(x, turn)


def exchange(x, a, b):
    low = iota((8, x.shape[1]), 0) < 4

    def tile(i, j):
        n = (i * b + j) * 4
        return x[n : n + 8]

    parts = []
    for j in range(0, b, 2):
        pairs = [(tile(i, j), tile(i + 1, j)) for i in range(0, a, 2)]
        parts += [jnp.where(low, u, pltpu.roll(v, 4, 0)) for u, v in pairs]
        parts += [jnp.where(low, pltpu.roll(u, 4, 0), v) for u, v in pairs]
    return jnp.concatenate(parts, axis=0)


def spread(h, par):
    r, f = iota((128, 512), 0), iota((128, 512), 1)
    device = ((f >> 7) << 1) + (((f >> 6) & 1) ^ h)
    k = (device << 3) + ((((f >> 5) & 1) ^ par) << 2) + ((f >> 3) & 3)
    return (r == k + h * 64).astype(F32).astype(BF)


def same_block(shape):
    return (iota(shape, 0) >> 6) == (iota(shape, 1) & 7)


def fetch_kernel(x_hbm, after_ref, out_ref, sem):
    @pl.when(core() == 0)
    def _():
        copy = pltpu.make_async_copy(x_hbm, out_ref, sem)
        copy.start()
        copy.wait()


def fetch(x, after):
    return pl.pallas_call(
        fetch_kernel,
        in_specs=[pl.BlockSpec(memory_space=pltpu.HBM), pl.BlockSpec()],
        out_shape=pltpu.VMEM(x.shape, BF),
        scratch_shapes=[pltpu.SemaphoreType.DMA],
        compiler_params=params(8),
        cost_estimate=cost(0, 8 * MIB),
        name="fetch",
    )(in_hbm(x), after)


def mix_body(x_ref, g_ref, out_ref, back_ref):
    par = parity()
    packed = jnp.concatenate(
        [g_ref[n, c * 96 + 64 : c * 96 + 96, :].astype(F32) for n in range(8) for c in range(2)],
        axis=0,
    )
    ordered = exchange(packed, 16, 8).astype(BF)
    for h in range(2):
        full = dot(ordered, spread(h, par))
        back_ref[h] = jnp.where(same_block((512, 512)), full, 0.0).astype(BF)
    lane_k = (iota((128, 512), 1) >> 3) & 3
    mixed = []
    for kh in range(2):
        rows = []
        for p in range(4):
            for g in range(4):
                n, k = chip(p, g, kh), kh * 32
                low, high = g_ref[n, k : k + 32, :], g_ref[n, k + 96 : k + 128, :]
                rows.append(jnp.where(par == (g >> 1), low.astype(F32), high.astype(F32)))
        turned = jnp.concatenate(rows, axis=0).T
        big = jnp.concatenate([jnp.where(lane_k == k, turned, 0.0) for k in range(4)], axis=0)
        mixed.append(dot(x_ref[:, kh * 512 : (kh + 1) * 512], big.astype(BF)).astype(BF))
    even = ((iota((mixed[0].shape[0], 128), 1) >> 5) & 1) == 0
    for p in range(4):
        lanes = slice(p * 128, (p + 1) * 128)
        a, b = mixed[0][:, lanes], mixed[1][:, lanes]
        out_ref[2 * p] = jnp.where(even, a, b)
        out_ref[2 * p + 1] = jnp.where(even, b, a)


def mix_kernel(x_hbm, x_ref, all_ref, near_ref, far_ref, out_ref, back_ref, g_ref, late_ref, sem):
    @pl.when(core() == 0)
    def _():
        mix_body(x_ref, all_ref, out_ref, back_ref)

    @pl.when(core() == 1)
    def _():
        copy = pltpu.make_async_copy(x_hbm, late_ref, sem)
        copy.start()
        here = plane()
        for z in range(4):
            g_ref[2 * z + here] = near_ref[z]
            g_ref[2 * z + 1 - here] = far_ref[z]
        copy.wait()
        mix_body(late_ref, g_ref, out_ref, back_ref)


def mix(tokens, x, gathered, near, far):
    rows = x.shape[0]
    return pl.pallas_call(
        mix_kernel,
        out_shape=(
            jax.ShapeDtypeStruct((8, rows, 128), BF),
            jax.ShapeDtypeStruct((2, 512, 512), BF),
        ),
        in_specs=[pl.BlockSpec(memory_space=pltpu.HBM)] + [pl.BlockSpec()] * 4,
        scratch_shapes=[
            pltpu.VMEM((8, 192, 128), BF),
            pltpu.VMEM(x.shape, BF),
            pltpu.SemaphoreType.DMA,
        ],
        compiler_params=params(),
        cost_estimate=cost(rows * 1024 * 1024, 4 * rows * 1024),
        name="mix",
    )(in_hbm(tokens), x, gathered, near, far)


def left_terms(grads, turned, left_ref):
    par = parity()
    total = jnp.zeros((512, 128), F32)
    for h in range(2):
        full = dot(grads[h], turned[h], ((0,), (0,)))
        full = jnp.where(same_block((512, 512)), full, 0.0).astype(BF)
        total = total + dot(full, spread(h, par), ((1,), (1,)))
    ordered = exchange(total, 8, 16)
    for s in range(16):
        left_ref[s] = ordered[s * 32 : (s + 1) * 32, :]


def middle_kernel(in_ref, back_ref, target_ref, student_ref, left_ref, out_ref, grad_ref):
    def work(later):
        turned = halves([in_ref[j] for j in range(8)])
        outs, grads = [], []
        for h in range(2):
            lanes = slice(h * 512, (h + 1) * 512)
            v = dot(turned[h], back_ref[h], ((1,), (1,)))
            square = v * v
            p = 0.5 + 0.5 * jnp.tanh(v * (ROOT + (ROOT * CUBE) * square))
            act = v * p
            slope = p + (act - act * p) * (2.0 * ROOT + (6.0 * ROOT * CUBE) * square)
            student_ref[:, lanes] = act.astype(BF)
            grad = ((act - target_ref[:, lanes].astype(F32)) * slope).astype(BF)
            outs.append(dot(grad, back_ref[h]).astype(BF))
            grads.append(grad)
            if not later:
                grad_ref[:, lanes] = grad
        low = iota((outs[0].shape[0], 128), 1) < 64
        for p in range(4):
            lanes = slice(p * 128, (p + 1) * 128)
            a, b = outs[0][:, lanes], outs[1][:, lanes]
            out_ref[2 * p] = jnp.where(low, a, b)
            out_ref[2 * p + 1] = jnp.where(low, b, a)
        if later:
            left_terms(grads, turned, left_ref)

    pl.when(core() == 0)(lambda: work(False))
    pl.when(core() == 1)(lambda: work(True))


def middle(received, back, target):
    rows = target.shape[0]
    return pl.pallas_call(
        middle_kernel,
        out_shape=(
            pltpu.VMEM((rows, 1024), BF),
            jax.ShapeDtypeStruct((16, 32, 128), F32),
            jax.ShapeDtypeStruct((8, rows, 128), BF),
            pltpu.VMEM((rows, 1024), BF),
        ),
        compiler_params=params(),
        cost_estimate=cost(2 * rows * 1024 * 1024, 10 * rows * 1024),
        name="middle",
    )(received, back, target)


def grads_kernel(
    student_ref, left_in, grad_ref, in_ref, back_ref, x_ref,
    student_hbm, mine_ref, other_ref, left_ref, sem,
):
    copy = pltpu.make_async_copy(student_ref, student_hbm, sem)
    copy.start()
    same = flip() == 0
    returned = split([back_ref[j] for j in range(8)])
    row_k = (iota((512, 128), 0) >> 3) & 3
    for kh in range(2):
        full = dot(returned[kh], x_ref[:, kh * 512 : (kh + 1) * 512], ((0,), (0,)))
        kept = jnp.zeros((512, 128), F32)
        for k in range(4):
            kept = jnp.where(row_k == k, full[:, k * 128 : (k + 1) * 128], kept)
        for p in range(4):
            for g in range(2):
                n = (p * 4 + g) * 32
                a, b = kept[n : n + 32], kept[n + 64 : n + 96]
                place = (chip(p, g, kh), slice(kh * 32, kh * 32 + 32))
                mine_ref[place] = jnp.where(same, a, b)
                other_ref[place] = jnp.where(same, b, a).astype(BF)
    @pl.when(core() == 0)
    def _():
        turned = halves([in_ref[j] for j in range(8)])
        left_terms([grad_ref[:, :512], grad_ref[:, 512:]], turned, left_ref)

    @pl.when(core() == 1)
    def _():
        left_ref[...] = left_in[...]

    for n in range(8):
        mine_ref[n, 64:96, :] = left_ref[2 * n + core()]
        other_ref[n, 64:96, :] = left_ref[2 * n + 1 - core()].astype(BF)
    copy.wait()


def grads(student, left, grad, received, returned, x):
    rows = x.shape[0]
    return pl.pallas_call(
        grads_kernel,
        out_shape=(
            pltpu.HBM(student.shape, BF),
            jax.ShapeDtypeStruct((8, 96, 128), F32),
            jax.ShapeDtypeStruct((8, 96, 128), BF),
        ),
        out_specs=(pl.BlockSpec(memory_space=pltpu.HBM), pl.BlockSpec(), pl.BlockSpec()),
        scratch_shapes=[pltpu.VMEM((16, 32, 128), F32), pltpu.SemaphoreType.DMA],
        compiler_params=params(),
        cost_estimate=cost(2 * rows * 1024 * 1024, 8 * rows * 1024),
        name="grads",
    )(student, left, grad, received, returned, x)


def sum_kernel(scale, in_ref, right_ref, left_ref):
    total = in_ref[0].astype(F32)
    for s in range(1, 8):
        total = total + in_ref[s].astype(F32)
    total = total * scale
    right_ref[...] = total[:64].reshape(8, 8, 128)
    left = total[64:]
    left_ref[:8] = left[:, :64].reshape(8, 4, 64)
    left_ref[8:] = left[:, 64:].reshape(8, 4, 64)


def sums(terms, scale):
    return pl.pallas_call(
        functools.partial(sum_kernel, scale),
        out_shape=(
            jax.ShapeDtypeStruct((8, 8, 128), F32),
            jax.ShapeDtypeStruct((16, 4, 64), F32),
        ),
        compiler_params=params(),
        name="sums",
    )(terms)


def shards(tokens, right_factor, left_factor, target):
    rows = tokens.shape[0]
    scale = 1.0 / math.sqrt(rows * lax.axis_size("seq"))
    chips = [[2 * n + c for n in range(8)] for c in range(2)]
    across = [(n, n ^ 1) for n in range(16)]
    own = pack(right_factor, left_factor)
    x = fetch(tokens, own)
    share = pair(own, lax.ppermute(own, "seq", across), x)

    def gather(share):
        return lax.all_to_all(share, "seq", 0, 0, tiled=True, axis_index_groups=chips)

    def gather_z(share):
        lines = [[4 * z + n for z in range(4)] for n in range(4)]
        return lax.all_to_all(share, "seq", 0, 0, tiled=True, axis_index_groups=lines)

    first = lax.axis_index("seq") % 2 == 0
    gathered = lax.cond(first, gather, lambda share: share, share)
    far = lax.ppermute(other_half(gathered), "seq", [(2 * n, 2 * n + 1) for n in range(8)])
    near = lax.cond(first, lambda share: share, gather_z, pass_on(share[:4], far))
    mixed, back = mix(tokens, x, gathered, near, far)
    received = lax.all_to_all(mixed, "blk", 0, 0, tiled=True)
    student, left, out, grad = middle(received, back, target)
    returned = lax.all_to_all(out, "blk", 0, 0, tiled=True)
    student, mine, other = grads(student, left, grad, received, returned, tokens)
    terms = (mine + lax.ppermute(other, "seq", across).astype(F32)).astype(BF)
    terms = lax.all_to_all(terms, "seq", 0, 0, tiled=True, axis_index_groups=chips)
    right_grad, left_grad = sums(terms, scale)
    return (student, right_grad, left_grad)


def solution(mesh):
    return jax.shard_map(
        shards,
        mesh=mesh,
        in_specs=(P("seq", "blk"), P("blk", "seq", None), P("blk", "seq", None), P("seq", "blk")),
        out_specs=(P("seq", "blk"), P("blk", "seq", None), P("blk", "seq", None)),
        check_vma=False,
    )
```

```python
import functools
import math

import jax
import jax.numpy as jnp
from jax import lax
from jax.experimental import pallas as pl
from jax.experimental.pallas import tpu as pltpu
from jax.sharding import PartitionSpec as P

BF = jnp.bfloat16
F32 = jnp.float32
MIB = 1 << 20
ROOT = math.sqrt(2.0 / math.pi)
CUBE = 0.044715


def iota(shape, dim):
    return lax.broadcasted_iota(jnp.int32, shape, dim)


def dot(a, b, dims=((1,), (0,))):
    return lax.dot_general(a, b, (dims, ((), ())), preferred_element_type=F32)


def params(limit=24):
    return pltpu.CompilerParams(vmem_limit_bytes=limit * MIB)


def cost(flops, size):
    return pl.CostEstimate(flops=int(flops), bytes_accessed=int(size), transcendentals=0)


def in_hbm(x):
    return pltpu.with_memory_space_constraint(x, pltpu.HBM)


def parity():
    return lax.rem(lax.axis_index("blk"), 2)


def joined(parts):
    return jnp.concatenate(parts, axis=1)


def halves(blocks):
    low = iota(blocks[0].shape, 1) < 64
    first = joined([jnp.where(low, blocks[2 * p], blocks[2 * p + 1]) for p in range(4)])
    second = joined([jnp.where(low, blocks[2 * p + 1], blocks[2 * p]) for p in range(4)])
    return first, second


def split(blocks):
    even = ((iota(blocks[0].shape, 1) >> 5) & 1) == 0
    first = joined([jnp.where(even, blocks[2 * p], blocks[2 * p + 1]) for p in range(4)])
    second = joined([jnp.where(even, blocks[2 * p + 1], blocks[2 * p]) for p in range(4)])
    return first, second


def chip(pair, g, kh):
    return 2 * pair + ((g & 1) ^ kh)


def core():
    return lax.rem(lax.axis_index("seq"), 2)


def flip():
    return lax.rem(lax.axis_index("seq") + lax.axis_index("blk"), 2)


def pack_kernel(right_hbm, left_hbm, out_ref, right_ref, left_ref, sems):
    copies = [
        pltpu.make_async_copy(right_hbm, right_ref, sems.at[0]),
        pltpu.make_async_copy(left_hbm, left_ref, sems.at[1]),
    ]
    for copy in copies:
        copy.start()
    for copy in copies:
        copy.wait()
    right = right_ref[...].astype(F32).reshape(64, 128)
    left = left_ref[...].astype(F32).reshape(64, 64)
    whole = jnp.concatenate([right, joined([left[:32], left[32:]])], axis=0).astype(BF)
    out_ref[...] = whole


def pack(right, left):
    return pl.pallas_call(
        pack_kernel,
        in_specs=[pl.BlockSpec(memory_space=pltpu.HBM)] * 2,
        out_shape=jax.ShapeDtypeStruct((96, 128), BF),
        scratch_shapes=[
            pltpu.VMEM(right.shape, BF),
            pltpu.VMEM(left.shape, BF),
            pltpu.SemaphoreType.DMA((2,)),
        ],
        compiler_params=params(),
        name="pack",
    )(in_hbm(right), in_hbm(left))


def pair_kernel(own_ref, sib_ref, after_ref, out_ref):
    first = core() == 0
    own, sib = own_ref[...].astype(F32), sib_ref[...].astype(F32)
    low, high = jnp.where(first, own, sib).astype(BF), jnp.where(first, sib, own).astype(BF)
    for n in range(8):
        out_ref[n, 0:96, :] = low
        out_ref[n, 96:192, :] = high


def pair(own, sibling, after):
    return pl.pallas_call(
        pair_kernel,
        in_specs=[pl.BlockSpec(), pl.BlockSpec(), pl.BlockSpec(memory_space=pl.ANY)],
        out_shape=jax.ShapeDtypeStruct((8, 192, 128), BF),
        compiler_params=params(8),
        name="pair",
    )(own, sibling, after)


def plane():
    return lax.rem(lax.div(lax.axis_index("seq"), 2), 2)


def other_kernel(g_ref, out_ref):
    there = 1 - plane()
    for z in range(4):
        out_ref[z] = g_ref[2 * z + there]


def other_half(gathered):
    return pl.pallas_call(
        other_kernel,
        out_shape=jax.ShapeDtypeStruct((4, 192, 128), BF),
        compiler_params=params(8),
        name="other_half",
    )(gathered)


def pass_kernel(x_ref, turn_ref, out_ref):
    pass


def pass_on(x, turn):
    return pl.pallas_call(
        pass_kernel,
        out_shape=jax.ShapeDtypeStruct(x.shape, x.dtype),
        in_specs=[pl.BlockSpec(memory_space=pl.ANY)] * 2,
        out_specs=pl.BlockSpec(memory_space=pl.ANY),
        input_output_aliases={0: 0},
        compiler_params=params(8),
        name="pass_on",
    )(x, turn)


def exchange(x, a, b):
    low = iota((8, x.shape[1]), 0) < 4

    def tile(i, j):
        n = (i * b + j) * 4
        return x[n : n + 8]

    parts = []
    for j in range(0, b, 2):
        pairs = [(tile(i, j), tile(i + 1, j)) for i in range(0, a, 2)]
        parts += [jnp.where(low, u, pltpu.roll(v, 4, 0)) for u, v in pairs]
        parts += [jnp.where(low, pltpu.roll(u, 4, 0), v) for u, v in pairs]
    return jnp.concatenate(parts, axis=0)


def spread(h, par):
    r, f = iota((128, 512), 0), iota((128, 512), 1)
    device = ((f >> 7) << 1) + (((f >> 6) & 1) ^ h)
    k = (device << 3) + ((((f >> 5) & 1) ^ par) << 2) + ((f >> 3) & 3)
    return (r == k + h * 64).astype(F32).astype(BF)


def same_block(shape):
    return (iota(shape, 0) >> 6) == (iota(shape, 1) & 7)


def fetch_kernel(x_hbm, after_ref, out_ref, sem):
    @pl.when(core() == 0)
    def _():
        copy = pltpu.make_async_copy(x_hbm, out_ref, sem)
        copy.start()
        copy.wait()


def fetch(x, after):
    return pl.pallas_call(
        fetch_kernel,
        in_specs=[pl.BlockSpec(memory_space=pltpu.HBM), pl.BlockSpec()],
        out_shape=pltpu.VMEM(x.shape, BF),
        scratch_shapes=[pltpu.SemaphoreType.DMA],
        compiler_params=params(8),
        cost_estimate=cost(0, 8 * MIB),
        name="fetch",
    )(in_hbm(x), after)


def back_body(g_ref, back_ref):
    par = parity()
    packed = jnp.concatenate(
        [g_ref[n, c * 96 + 64 : c * 96 + 96, :].astype(F32) for n in range(8) for c in range(2)],
        axis=0,
    )
    ordered = exchange(packed, 16, 8).astype(BF)
    for h in range(2):
        full = dot(ordered, spread(h, par))
        back_ref[h] = jnp.where(same_block((512, 512)), full, 0.0).astype(BF)


def mix_body(x_ref, g_ref, out_ref):
    par = parity()
    lane_k = (iota((128, 512), 1) >> 3) & 3
    mixed = []
    for kh in range(2):
        rows = []
        for p in range(4):
            for g in range(4):
                n, k = chip(p, g, kh), kh * 32
                low, high = g_ref[n, k : k + 32, :], g_ref[n, k + 96 : k + 128, :]
                rows.append(jnp.where(par == (g >> 1), low.astype(F32), high.astype(F32)))
        turned = jnp.concatenate(rows, axis=0).T
        big = jnp.concatenate([jnp.where(lane_k == k, turned, 0.0) for k in range(4)], axis=0)
        mixed.append(dot(x_ref[:, kh * 512 : (kh + 1) * 512], big.astype(BF)).astype(BF))
    even = ((iota((mixed[0].shape[0], 128), 1) >> 5) & 1) == 0
    for p in range(4):
        lanes = slice(p * 128, (p + 1) * 128)
        a, b = mixed[0][:, lanes], mixed[1][:, lanes]
        out_ref[2 * p] = jnp.where(even, a, b)
        out_ref[2 * p + 1] = jnp.where(even, b, a)


def mix_kernel(x_hbm, x_ref, all_ref, near_ref, far_ref, out_ref, back_ref, g_ref, late_ref, sem):
    @pl.when(core() == 0)
    def _():
        mix_body(x_ref, all_ref, out_ref)
        back_body(all_ref, back_ref)

    @pl.when(core() == 1)
    def _():
        copy = pltpu.make_async_copy(x_hbm, late_ref, sem)
        copy.start()
        here = plane()
        for z in range(4):
            g_ref[2 * z + here] = near_ref[z]
            g_ref[2 * z + 1 - here] = far_ref[z]
        back_body(g_ref, back_ref)
        copy.wait()
        mix_body(late_ref, g_ref, out_ref)


def mix(tokens, x, gathered, near, far):
    rows = x.shape[0]
    return pl.pallas_call(
        mix_kernel,
        out_shape=(
            jax.ShapeDtypeStruct((8, rows, 128), BF),
            jax.ShapeDtypeStruct((2, 512, 512), BF),
        ),
        in_specs=[pl.BlockSpec(memory_space=pltpu.HBM)] + [pl.BlockSpec()] * 4,
        scratch_shapes=[
            pltpu.VMEM((8, 192, 128), BF),
            pltpu.VMEM(x.shape, BF),
            pltpu.SemaphoreType.DMA,
        ],
        compiler_params=params(),
        cost_estimate=cost(rows * 1024 * 1024, 4 * rows * 1024),
        name="mix",
    )(in_hbm(tokens), x, gathered, near, far)


def left_terms(grads, turned, left_ref):
    par = parity()
    total = jnp.zeros((512, 128), F32)
    for h in range(2):
        full = dot(grads[h], turned[h], ((0,), (0,)))
        full = jnp.where(same_block((512, 512)), full, 0.0).astype(BF)
        total = total + dot(full, spread(h, par), ((1,), (1,)))
    ordered = exchange(total, 8, 16)
    for s in range(16):
        left_ref[s] = ordered[s * 32 : (s + 1) * 32, :]


def middle_kernel(in_ref, back_ref, target_ref, student_ref, left_ref, out_ref, grad_ref):
    def work(later):
        turned = halves([in_ref[j] for j in range(8)])
        outs, grads = [], []
        for h in range(2):
            lanes = slice(h * 512, (h + 1) * 512)
            v = dot(turned[h], back_ref[h], ((1,), (1,)))
            square = v * v
            p = 0.5 + 0.5 * jnp.tanh(v * (ROOT + (ROOT * CUBE) * square))
            act = v * p
            slope = p + (act - act * p) * (2.0 * ROOT + (6.0 * ROOT * CUBE) * square)
            student_ref[:, lanes] = act.astype(BF)
            grad = ((act - target_ref[:, lanes].astype(F32)) * slope).astype(BF)
            outs.append(dot(grad, back_ref[h]).astype(BF))
            grads.append(grad)
            if not later:
                grad_ref[:, lanes] = grad
        low = iota((outs[0].shape[0], 128), 1) < 64
        for p in range(4):
            lanes = slice(p * 128, (p + 1) * 128)
            a, b = outs[0][:, lanes], outs[1][:, lanes]
            out_ref[2 * p] = jnp.where(low, a, b)
            out_ref[2 * p + 1] = jnp.where(low, b, a)
        if later:
            left_terms(grads, turned, left_ref)

    pl.when(core() == 0)(lambda: work(False))
    pl.when(core() == 1)(lambda: work(True))


def middle(received, back, target):
    rows = target.shape[0]
    return pl.pallas_call(
        middle_kernel,
        out_shape=(
            pltpu.VMEM((rows, 1024), BF),
            jax.ShapeDtypeStruct((16, 32, 128), F32),
            jax.ShapeDtypeStruct((8, rows, 128), BF),
            pltpu.VMEM((rows, 1024), BF),
        ),
        compiler_params=params(),
        cost_estimate=cost(2 * rows * 1024 * 1024, 10 * rows * 1024),
        name="middle",
    )(received, back, target)


def grads_kernel(
    student_ref, left_in, grad_ref, in_ref, back_ref, x_ref,
    student_hbm, mine_ref, other_ref, left_ref, sem,
):
    copy = pltpu.make_async_copy(student_ref, student_hbm, sem)
    copy.start()
    same = flip() == 0
    returned = split([back_ref[j] for j in range(8)])
    row_k = (iota((512, 128), 0) >> 3) & 3
    for kh in range(2):
        full = dot(returned[kh], x_ref[:, kh * 512 : (kh + 1) * 512], ((0,), (0,)))
        kept = jnp.zeros((512, 128), F32)
        for k in range(4):
            kept = jnp.where(row_k == k, full[:, k * 128 : (k + 1) * 128], kept)
        for p in range(4):
            for g in range(2):
                n = (p * 4 + g) * 32
                a, b = kept[n : n + 32], kept[n + 64 : n + 96]
                place = (chip(p, g, kh), slice(kh * 32, kh * 32 + 32))
                mine_ref[place] = jnp.where(same, a, b)
                other_ref[place] = jnp.where(same, b, a).astype(BF)
    @pl.when(core() == 0)
    def _():
        turned = halves([in_ref[j] for j in range(8)])
        left_terms([grad_ref[:, :512], grad_ref[:, 512:]], turned, left_ref)

    @pl.when(core() == 1)
    def _():
        left_ref[...] = left_in[...]

    for n in range(8):
        mine_ref[n, 64:96, :] = left_ref[2 * n + core()]
        other_ref[n, 64:96, :] = left_ref[2 * n + 1 - core()].astype(BF)
    copy.wait()


def grads(student, left, grad, received, returned, x):
    rows = x.shape[0]
    return pl.pallas_call(
        grads_kernel,
        out_shape=(
            pltpu.HBM(student.shape, BF),
            jax.ShapeDtypeStruct((8, 96, 128), F32),
            jax.ShapeDtypeStruct((8, 96, 128), BF),
        ),
        out_specs=(pl.BlockSpec(memory_space=pltpu.HBM), pl.BlockSpec(), pl.BlockSpec()),
        scratch_shapes=[pltpu.VMEM((16, 32, 128), F32), pltpu.SemaphoreType.DMA],
        compiler_params=params(),
        cost_estimate=cost(2 * rows * 1024 * 1024, 8 * rows * 1024),
        name="grads",
    )(student, left, grad, received, returned, x)


def sum_kernel(scale, in_ref, right_ref, left_ref):
    total = in_ref[0].astype(F32)
    for s in range(1, 8):
        total = total + in_ref[s].astype(F32)
    total = total * scale
    right_ref[...] = total[:64].reshape(8, 8, 128)
    left = total[64:]
    left_ref[:8] = left[:, :64].reshape(8, 4, 64)
    left_ref[8:] = left[:, 64:].reshape(8, 4, 64)


def sums(terms, scale):
    return pl.pallas_call(
        functools.partial(sum_kernel, scale),
        out_shape=(
            jax.ShapeDtypeStruct((8, 8, 128), F32),
            jax.ShapeDtypeStruct((16, 4, 64), F32),
        ),
        compiler_params=params(),
        name="sums",
    )(terms)


def shards(tokens, right_factor, left_factor, target):
    rows = tokens.shape[0]
    scale = 1.0 / math.sqrt(rows * lax.axis_size("seq"))
    chips = [[2 * n + c for n in range(8)] for c in range(2)]
    across = [(n, n ^ 1) for n in range(16)]
    own = pack(right_factor, left_factor)
    x = fetch(tokens, own)
    share = pair(own, lax.ppermute(own, "seq", across), x)

    def gather(share):
        return lax.all_to_all(share, "seq", 0, 0, tiled=True, axis_index_groups=chips)

    def gather_z(share):
        lines = [[4 * z + n for z in range(4)] for n in range(4)]
        return lax.all_to_all(share, "seq", 0, 0, tiled=True, axis_index_groups=lines)

    first = lax.axis_index("seq") % 2 == 0
    gathered = lax.cond(first, gather, lambda share: share, share)
    far = lax.ppermute(other_half(gathered), "seq", [(2 * n, 2 * n + 1) for n in range(8)])
    near = lax.cond(first, lambda share: share, gather_z, pass_on(share[:4], far))
    mixed, back = mix(tokens, x, gathered, near, far)
    received = lax.all_to_all(mixed, "blk", 0, 0, tiled=True)
    student, left, out, grad = middle(received, back, target)
    returned = lax.all_to_all(out, "blk", 0, 0, tiled=True)
    student, mine, other = grads(student, left, grad, received, returned, tokens)
    terms = (mine + lax.ppermute(other, "seq", across).astype(F32)).astype(BF)
    terms = lax.all_to_all(terms, "seq", 0, 0, tiled=True, axis_index_groups=chips)
    right_grad, left_grad = sums(terms, scale)
    return (student, right_grad, left_grad)


def solution(mesh):
    return jax.shard_map(
        shards,
        mesh=mesh,
        in_specs=(P("seq", "blk"), P("blk", "seq", None), P("blk", "seq", None), P("seq", "blk")),
        out_specs=(P("seq", "blk"), P("blk", "seq", None), P("blk", "seq", None)),
        check_vma=False,
    )
```
